512 devices in a mesh: section: 8 (over y_lo, x), ctx: 64 (over y_hi, z, core).
Axes of the slice: x: 4, y: 8 (y_hi: 4, y_lo: 2; y = y_hi * 2 + y_lo), z: 8, core: 2. Of those that a mesh axis runs over, the one named last changes fastest.
Arguments:
- x_in: bfloat16 [2048, 1536], P('ctx'), may hold values from -6 to 6
- stale_inputs: bfloat16 [8, 2048, 1536], P('section', 'ctx'), may hold values from -6 to 6
- w_query: bfloat16 [8, 12, 128, 128], P('section'), may hold values from -0.5 to 0.5
- w_key: bfloat16 [8, 12, 128, 128], P('section'), may hold values from -0.5 to 0.5
- w_value: bfloat16 [8, 12, 128, 128], P('section'), may hold values from -0.5 to 0.5
- w_out: bfloat16 [8, 12, 128, 128], P('section'), may hold values from -0.5 to 0.5
- score_scale: float32 [8, 12], P('section'), may hold values from 1 to 3
- assign: int32 [2048], P('ctx'), may hold values from 0 to 3, as said below
Outputs:
- section_out: bfloat16 [8, 2048, 1536], P('section', 'ctx')
The draws below stay inside these ranges and needn't reach their ends.
Inputs may be any that keep to these rules, and one draw needn't show every extreme that they name: `assign`: each aligned block of 32 tokens holds the same number of tokens of every micro-batch.
All inputs are finite; a program needn't handle non-finite values.
Results may differ from the reference program's by a relative error of at most 0.013.
Values may be sent and summed in bfloat16 or wider, within the bound.
A program may use at most 128 MiB of HBM per device.

```python
import math
import jax
import jax.numpy as jnp
from jax import lax

HEADS = 12
HD = 128
MB = 4
TOK_DEV = 32
HW = 1536
TOKENS = 2048
N_SECTION = 8


def draw_assign(key, part):
    tile_keys = jax.random.split(key, TOKENS // TOK_DEV)
    shuffled = jax.vmap(lambda tile_key: jax.random.permutation(tile_key, TOK_DEV))(tile_keys)
    return (shuffled // (TOK_DEV // MB)).reshape(-1).astype(jnp.int32)


def steps_of(own_key, dims, pieces, smallest, largest):
    gain = 1.0
    for position, shards_of in pieces:
        heights = jax.random.uniform(jax.random.fold_in(jax.random.fold_in(own_key, 6), position), (shards_of,), jnp.float32, smallest / len(pieces), largest / len(pieces))
        gain = gain * jnp.repeat(jnp.exp(heights), dims[position] // shards_of).reshape((-1,) + (1,) * (len(dims) - 1 - position))
    return gain


def scatter_about(own_key, dims, width, bound, shards=(), kind=jnp.bfloat16):
    array = jax.random.normal(own_key, dims, jnp.float32) * width
    if len(shards) > 0:
        array = steps_of(own_key, dims, shards, -0.22, 0.18) * array
    return jnp.clip(array, min=-bound, max=bound).astype(kind)


def setup_inputs(seed: int = 0) -> dict:
    seeds = jax.random.split(jax.random.key(seed), 9)
    return {
        "x_in": scatter_about(seeds[0], (TOKENS, HW), 1.0, 6.0, ((0, 64),)),
        "stale_inputs": scatter_about(seeds[1], (N_SECTION, TOKENS, HW), 1.0, 6.0, ((0, 8), (1, 64))),
        "w_query": scatter_about(seeds[2], (N_SECTION, HEADS, HD, HD), HD ** -0.5, 0.5, ((0, 8),)),
        "w_key": scatter_about(seeds[3], (N_SECTION, HEADS, HD, HD), HD ** -0.5, 0.5, ((0, 8),)),
        "w_value": scatter_about(seeds[4], (N_SECTION, HEADS, HD, HD), HD ** -0.5, 0.5, ((0, 8),)),
        "w_out": scatter_about(seeds[5], (N_SECTION, HEADS, HD, HD), HD ** -0.5, 0.5, ((0, 8),)),
        "score_scale": jnp.clip(jnp.exp(math.log(3.0) - 1.0986123 * jax.random.uniform(seeds[6], (N_SECTION, HEADS), jnp.float32) ** steps_of(seeds[6], (N_SECTION, HEADS), ((0, 8),), -0.2, 0.2)), 1.0, 3.0),
        "assign": draw_assign(jax.random.fold_in(seeds[8], 71), 0),
    }


def normalize(values):
    floats = values.astype(jnp.float32)
    return floats * lax.rsqrt(lax.optimization_barrier(jnp.mean(floats * floats, axis=-1, keepdims=True)) + 1e-06)

def project(normed, weight):
    count = normed.shape[0]
    return jnp.einsum('nhd,hde->nhe', normed.astype(jnp.float32).reshape(count, HEADS, HD), weight.astype(jnp.float32))

def heads_of(normed, w_query, w_key, w_value, scales):
    queries = (normalize(project(normed, w_query)) * (scales[None, :, None] / math.sqrt(HD))).astype(jnp.bfloat16)
    keys = normalize(project(normed, w_key)).astype(jnp.bfloat16)
    values = project(normed, w_value).astype(jnp.bfloat16)
    return (queries, keys, values)

def layer(hidden, stale, w_query, w_key, w_value, w_out, scales, assign):
    normed = normalize(hidden).astype(jnp.bfloat16)
    queries, keys, values = heads_of(normed, w_query, w_key, w_value, scales)
    stale_normed = normalize(stale).astype(jnp.bfloat16)
    unused, stale_keys, stale_values = heads_of(stale_normed, w_query, w_key, w_value, scales)
    key_tile = jnp.arange(TOKENS, dtype=jnp.int32) // TOK_DEV
    stale_kf = stale_keys.astype(jnp.float32)
    stale_vf = stale_values.astype(jnp.float32)

    def one_tile(index):
        start = (index * TOK_DEV).astype(jnp.int32)
        tile_q = lax.dynamic_slice_in_dim(queries, start, TOK_DEV, 0).astype(jnp.float32)
        tile_k = lax.dynamic_slice_in_dim(keys, start, TOK_DEV, 0).astype(jnp.float32)
        tile_v = lax.dynamic_slice_in_dim(values, start, TOK_DEV, 0).astype(jnp.float32)
        tile_sk = lax.dynamic_slice_in_dim(stale_kf, start, TOK_DEV, 0)
        tile_sv = lax.dynamic_slice_in_dim(stale_vf, start, TOK_DEV, 0)
        tile_assign = lax.dynamic_slice_in_dim(assign, start, TOK_DEV, 0)
        far = (key_tile != index).astype(jnp.float32)
        chosen = (tile_assign[None, :] <= tile_assign[:, None]).astype(jnp.float32)
        e_far = jnp.exp(jnp.einsum('qhd,khd->hqk', tile_q, stale_kf)) * far[None, None, :]
        e_new = jnp.exp(jnp.einsum('qhd,khd->hqk', tile_q, tile_k)) * chosen[None]
        e_old = jnp.exp(jnp.einsum('qhd,khd->hqk', tile_q, tile_sk)) * (1.0 - chosen)[None]
        denom = lax.optimization_barrier(jnp.sum(e_far, -1)) + lax.optimization_barrier(jnp.sum(e_new, -1)) + lax.optimization_barrier(jnp.sum(e_old, -1))
        numer = jnp.einsum('hqk,khd->qhd', e_far.astype(jnp.bfloat16).astype(jnp.float32), stale_vf)
        numer = numer + jnp.einsum('hqk,khd->qhd', e_new.astype(jnp.bfloat16).astype(jnp.float32), tile_v)
        numer = numer + jnp.einsum('hqk,khd->qhd', e_old.astype(jnp.bfloat16).astype(jnp.float32), tile_sv)
        return (numer / jnp.transpose(denom)[:, :, None]).astype(jnp.bfloat16)
    attended = lax.map(one_tile, jnp.arange(TOKENS // TOK_DEV, dtype=jnp.int32))
    attended = attended.reshape(TOKENS, HEADS * HD)
    mixed = project(attended, w_out).reshape(TOKENS, HEADS * HD)
    return (hidden.astype(jnp.float32) + mixed).astype(jnp.bfloat16)

def reference(x_in, stale_inputs, w_query, w_key, w_value, w_out, score_scale, assign):
    hidden = x_in
    results = []
    for section in range(N_SECTION):
        hidden = layer(hidden, stale_inputs[section], w_query[section], w_key[section], w_value[section], w_out[section], score_scale[section], assign)
        results.append(hidden)
    return jnp.stack(results)
```

```python
import functools
import math

import jax
import jax.numpy as jnp
from jax import lax
from jax.experimental import pallas as pl
from jax.experimental.pallas import tpu as pltpu
from jax.sharding import PartitionSpec as P

F32 = jnp.float32
BF16 = jnp.bfloat16
MESH = pl.DeviceIdType.MESH
EPS = 1e-6
HD = 128
TILE = 32
QUAD = 4
TOK = QUAD * TILE
GRP = 3
FEAT = QUAD * GRP * HD


def nn(a, b):
    return lax.dot_general(a, b, (((1,), (0,)), ((), ())), preferred_element_type=F32)


def nt(a, b):
    return lax.dot_general(a, b, (((1,), (1,)), ((), ())), preferred_element_type=F32)


def tn(a, b):
    return lax.dot_general(a, b, (((0,), (0,)), ((), ())), preferred_element_type=F32)


def arrived(ref, sem):
    pltpu.make_async_copy(ref, ref, sem).wait()


def kernel(
    sections, nz,
    x_ref, stale_ref, wq_ref, wk_ref, wv_ref, wo_ref, scale_ref, assign_ref,
    out_ref,
    stv, wts, normed, near, mask, xin, wk3, wT, wvoT, keys, vals, ht, ot, ob, sumsq, sumsq_out,
    load_sem, xs_sem, xr_sem, ms_sem, mr_sem, qs_sem, qr_sem, ring_sem, sib_sem, near_sem,
    hs_sem, hr_sem, ss_sem, sr_sem, os_sem, or_sem,
):
    s = lax.axis_index("section")
    c = lax.axis_index("ctx")
    yh = c // (2 * nz)
    z = (c // 2) % nz
    core = c % 2
    half = nz // 2

    def at(section, y, zz, k):
        return (section, (y * nz + zz) * 2 + k)

    def peer(d):
        return (yh + d) % QUAD

    right = at(s, yh, (z + 1) % nz, core)
    left = at(s, yh, (z + nz - 1) % nz, core)
    sibling = at(s, yh, z, 1 - core)
    first = s == 0
    has_next = s < sections - 1
    mine = pl.ds(pl.multiple_of(yh * TILE, TILE), TILE)
    columns = pl.ds(pl.multiple_of(yh * (GRP * HD), GRP * HD), GRP * HD)

    def remote(src, dst, send, recv, device):
        return pltpu.make_async_remote_copy(
            src_ref=src, dst_ref=dst, send_sem=send, recv_sem=recv,
            device_id=device, device_id_type=MESH,
        )

    load_stale = pltpu.make_async_copy(stale_ref.at[0], stv, load_sem.at[0])
    load_stale.start()
    loads = []
    for i, w in enumerate((wk_ref, wq_ref, wv_ref, wo_ref)):
        loads.append(
            pltpu.make_async_copy(w.at[0, pl.ds(yh * GRP, GRP)], wts.at[i], load_sem.at[i + 1])
        )
        loads[-1].start()
    load_x = pltpu.make_async_copy(x_ref.at[:, columns], xin.at[mine, :], load_sem.at[5])

    @pl.when(first)
    def _():
        load_x.start()

    barrier = pltpu.get_barrier_semaphore()

    def greet(device):
        pl.semaphore_signal(barrier, inc=1, device_id=device, device_id_type=MESH)

    for d in range(1, QUAD):
        greet(at(s, peer(d), z, core))
    for device in (right, left, sibling):
        greet(device)

    @pl.when(has_next)
    def _():
        for d in range(QUAD):
            greet(at(s + 1, peer(d), z, core))

    @pl.when(s > 0)
    def _():
        for d in range(QUAD):
            greet(at(s - 1, peer(d), z, core))

    load_stale.wait()
    st = stv[...].astype(F32)
    n = (st * lax.rsqrt(jnp.mean(st * st, axis=-1, keepdims=True) + EPS)).astype(BF16)
    for h in range(QUAD * GRP):
        normed[h] = n[:, h * HD:(h + 1) * HD]
    near[0, 0, :, mine, :] = normed[pl.ds(yh * GRP, GRP)]

    row = assign_ref[...].astype(F32)
    row = jnp.concatenate([row] * QUAD, axis=1)
    lane = lax.broadcasted_iota(jnp.int32, (TILE, TOK), 1)
    sub = lax.broadcasted_iota(jnp.int32, (TILE, TOK), 0)
    rows = jnp.broadcast_to(row, (TILE, TOK))
    col = jnp.sum(jnp.where(lane == sub, rows, 0.0), axis=1, keepdims=True)
    fresh = jnp.where(col <= rows, 1.0, 0.0) * jnp.where(lane // TILE == yh, 1.0, 0.0)
    mask[mine, :] = fresh.astype(BF16)

    pl.semaphore_wait(
        barrier, 6 + QUAD * jnp.where(has_next, 1, 0) + QUAD * jnp.where(s > 0, 1, 0)
    )

    quad_sends, mask_sends, x_sends = [], [], []
    for d in range(1, QUAD):
        to = at(s, peer(d), z, core)
        quad_sends.append(remote(
            normed.at[pl.ds(peer(d) * GRP, GRP)], near.at[0, 0, :, mine, :],
            qs_sem.at[d - 1], qr_sem.at[d - 1], to,
        ))
        mask_sends.append(remote(
            mask.at[mine, :], mask.at[mine, :], ms_sem.at[d - 1], mr_sem.at[d - 1], to,
        ))
        x_sends.append(remote(
            x_ref.at[:, pl.ds(pl.multiple_of(peer(d) * (GRP * HD), GRP * HD), GRP * HD)],
            xin.at[mine, :], xs_sem.at[d - 1], xr_sem.at[d - 1], to,
        ))
    for copy in quad_sends:
        copy.start()

    @pl.when(first)
    def _():
        for copy in x_sends:
            copy.start()

    for copy in mask_sends:
        copy.start()

    for copy in loads:
        copy.wait()
    for h in range(GRP):
        wk = wts[0, h]
        wk3[h] = wk
        wvo = nn(wts[2, h], wts[3, h]).T.astype(BF16)
        wvoT[h] = wvo
        wT[h, 0:HD, :] = wts[1, h].astype(F32).T.astype(BF16)
        wT[h, HD:2 * HD, :] = wk.astype(F32).T.astype(BF16)
        wT[h, 2 * HD:, :] = wvo

    def to_right(t, h):
        return remote(
            near.at[(nz - t) % nz, 0, h], near.at[nz - t - 1, 0, h],
            ring_sem.at[0, t, h], near_sem.at[nz - t - 1, 0, h], right,
        )

    def to_left(t, h):
        return remote(
            near.at[t, 0, h], near.at[t + 1, 0, h],
            ring_sem.at[1, t, h], near_sem.at[t + 1, 0, h], left,
        )

    def to_sibling(r, h):
        return remote(
            near.at[r, 0, h], near.at[r, 1, h],
            sib_sem.at[r, h], near_sem.at[r, 1, h], sibling,
        )

    sends = []

    def start(copy):
        copy.start()
        sends.append(copy)

    def prepare(r, k):
        for h in range(GRP):
            block = near[r, k, h]
            raw = nn(block, wk3[h])
            scaled = raw * lax.rsqrt(jnp.mean(raw * raw, axis=-1, keepdims=True) + EPS)
            keys[h, r * TOK:(r + 1) * TOK, k * HD:(k + 1) * HD] = scaled.astype(BF16)
            vals[h, k * HD:(k + 1) * HD, r * TOK:(r + 1) * TOK] = nt(wvoT[h], block).astype(BF16)

    def sibling_slots(slots):
        for r in slots:
            for h in range(GRP):
                arrived(near.at[r, 1, h], near_sem.at[r, 1, h])
            prepare(r, 1)

    for d in range(1, QUAD):
        source = pl.ds(pl.multiple_of(((yh + QUAD - d) % QUAD) * TILE, TILE), TILE)
        arrived(near.at[0, 0, :, source, :], qr_sem.at[d - 1])
    for h in range(GRP):
        if half > 1 or h < 2:
            start(to_right(0, h))
        if half > 1 or h == 2:
            start(to_left(0, h))
        start(to_sibling(0, h))
    prepare(0, 0)
    before = [0]
    for t in range(1, half + 1):
        back = nz - t
        for h in range(GRP):
            arrived(near.at[back, 0, h], near_sem.at[back, 0, h])
            if t < half - 1 or (t == half - 1 and h < 2):
                start(to_right(t, h))
            start(to_sibling(back, h))
            if back != t:
                arrived(near.at[t, 0, h], near_sem.at[t, 0, h])
                if t < half - 1 or (t == half - 1 and h == 2):
                    start(to_left(t, h))
                start(to_sibling(t, h))
        sibling_slots(before)
        before = [back] if back == t else [back, t]
        for r in before:
            prepare(r, 0)
    sibling_slots(before)

    for d in range(1, QUAD):
        source = pl.ds(pl.multiple_of(((yh + QUAD - d) % QUAD) * TILE, TILE), TILE)
        arrived(mask.at[source, :], mr_sem.at[d - 1])

    def sum_to(section, d):
        return remote(
            sumsq_out, sumsq.at[d], ss_sem.at[d], sr_sem.at[d], at(section, peer(d), z, core)
        )

    def squares(values):
        return jnp.sum((values * values).reshape(HD // 8, 8, TOK), axis=0)

    @pl.when(first)
    def _():
        load_x.wait()
        for d in range(1, QUAD):
            source = pl.ds(pl.multiple_of(((yh + QUAD - d) % QUAD) * TILE, TILE), TILE)
            arrived(xin.at[source, :], xr_sem.at[d - 1])
        part = jnp.zeros((8, TOK), F32)
        for h in range(GRP):
            turned = xin[:, h * HD:(h + 1) * HD].astype(F32).T
            ht[h] = turned.astype(BF16)
            part = part + squares(turned)
        sumsq_out[...] = part
        sumsq[0] = part
        own = [sum_to(s, d) for d in range(1, QUAD)]
        for copy in own:
            copy.start()
        for copy in own:
            copy.wait_send()

    @pl.when(s > 0)
    def _():
        for h in range(GRP):
            arrived(ht.at[h], hr_sem.at[h])
        arrived(sumsq.at[0], sr_sem.at[0])

    for d in range(1, QUAD):
        arrived(sumsq.at[d], sr_sem.at[d])

    total = sumsq[0] + sumsq[1] + sumsq[2] + sumsq[3]
    mean_sq = jnp.sum(total, axis=0, keepdims=True) * (1.0 / FEAT) + EPS
    inv = lax.rsqrt(mean_sq)
    eps = EPS * mean_sq
    chosen = mask[...].astype(F32)
    keep = jnp.concatenate([1.0 - chosen, jnp.ones_like(chosen)], axis=1)
    zero = jnp.zeros((HD, TOK), BF16)

    def hand_on(h):
        return remote(ot.at[h], ht.at[h], hs_sem.at[h], hr_sem.at[h], at(s + 1, yh, z, core))

    part = jnp.zeros((8, TOK), F32)
    for h in range(GRP):
        hidden = ht[h]
        mapped = nn(wT[h], hidden)
        pq, pk, pv = mapped[0:HD], mapped[HD:2 * HD], mapped[2 * HD:]
        scale = scale_ref[0, yh * GRP + h] * (math.log2(math.e) / math.sqrt(HD))
        aq = lax.rsqrt(jnp.sum(pq * pq, axis=0, keepdims=True) * (1.0 / HD) + eps) * scale
        bk = lax.rsqrt(jnp.sum(pk * pk, axis=0, keepdims=True) * (1.0 / HD) + eps)
        q = (pq * aq).astype(BF16)
        kf = (pk * bk).astype(BF16)
        vf = (pv * inv).astype(BF16)
        pair = jnp.concatenate(
            [jnp.concatenate([q, zero], axis=1), jnp.concatenate([zero, q], axis=1)], axis=0
        )
        e = jnp.exp2(nn(keys[h], pair))
        e = jnp.concatenate([e[0:TOK] * keep, e[TOK:]], axis=0)
        e_new = jnp.exp2(tn(kf, q)) * chosen
        den = jnp.sum(e.reshape(nz * TOK // 8, 8, 2 * TOK), axis=0)
        den = den[:, :TOK] + den[:, TOK:] + jnp.sum(e_new.reshape(TOK // 8, 8, TOK), axis=0)
        den = jnp.sum(den, axis=0, keepdims=True)
        both = nn(vals[h], e.astype(BF16))
        numer = both[0:HD, 0:TOK] + both[HD:, TOK:] + nn(vf, e_new.astype(BF16))
        result = (hidden.astype(F32) + numer * (1.0 / den)).astype(BF16)
        ot[h] = result

        @pl.when(has_next)
        def _():
            hand_on(h).start()

        part = part + squares(result.astype(F32))

    @pl.when(has_next)
    def _():
        sumsq_out[...] = part
        for d in range(QUAD):
            sum_to(s + 1, d).start()

    for h in range(GRP):
        ob[:, h * HD:(h + 1) * HD] = ot[h].astype(F32).T.astype(BF16)
    own_out = pltpu.make_async_copy(ob.at[mine, :], out_ref.at[0, :, columns], load_sem.at[0])
    own_out.start()
    outs = []
    for d in range(1, QUAD):
        theirs = pl.ds(pl.multiple_of(peer(d) * TILE, TILE), TILE)
        outs.append(remote(
            ob.at[theirs, :], out_ref.at[0, :, columns],
            os_sem.at[d - 1], or_sem.at[d - 1], at(s, peer(d), z, core),
        ))
        outs[-1].start()

    for copy in sends + quad_sends + mask_sends:
        copy.wait_send()

    @pl.when(first)
    def _():
        for copy in x_sends:
            copy.wait_send()

    @pl.when(has_next)
    def _():
        for h in range(GRP):
            hand_on(h).wait_send()
        for d in range(QUAD):
            sum_to(s + 1, d).wait_send()

    own_out.wait()
    for d, copy in enumerate(outs, 1):
        copy.wait_send()
        theirs = pl.ds(
            pl.multiple_of(((yh + QUAD - d) % QUAD) * (GRP * HD), GRP * HD), GRP * HD
        )
        arrived(out_ref.at[0, :, theirs], or_sem.at[d - 1])


def solution(mesh):
    sections = mesh.shape["section"]
    nz = mesh.shape["ctx"] // (2 * QUAD)
    keys = nz * TOK

    def body(x_in, stale_inputs, w_query, w_key, w_value, w_out, score_scale, assign):
        anywhere = pl.BlockSpec(memory_space=pl.ANY)
        dma = pltpu.SemaphoreType.DMA
        return pl.pallas_call(
            functools.partial(kernel, sections, nz),
            out_shape=jax.ShapeDtypeStruct(stale_inputs.shape, BF16),
            in_specs=[anywhere] * 6 + [
                pl.BlockSpec(memory_space=pltpu.SMEM),
                pl.BlockSpec(memory_space=pltpu.VMEM),
            ],
            out_specs=anywhere,
            scratch_shapes=[
                pltpu.VMEM((TILE, FEAT), BF16),
                pltpu.VMEM((4, GRP, HD, HD), BF16),
                pltpu.VMEM((QUAD * GRP, TILE, HD), BF16),
                pltpu.VMEM((nz, 2, GRP, TOK, HD), BF16),
                pltpu.VMEM((TOK, TOK), BF16),
                pltpu.VMEM((TOK, GRP * HD), BF16),
                pltpu.VMEM((GRP, HD, HD), BF16),
                pltpu.VMEM((GRP, 3 * HD, HD), BF16),
                pltpu.VMEM((GRP, HD, HD), BF16),
                pltpu.VMEM((GRP, keys, 2 * HD), BF16),
                pltpu.VMEM((GRP, 2 * HD, keys), BF16),
                pltpu.VMEM((GRP, HD, TOK), BF16),
                pltpu.VMEM((GRP, HD, TOK), BF16),
                pltpu.VMEM((TOK, GRP * HD), BF16),
                pltpu.VMEM((QUAD, 8, TOK), F32),
                pltpu.VMEM((8, TOK), F32),
                dma((6,)),
                dma((3,)), dma((3,)),
                dma((3,)), dma((3,)),
                dma((3,)), dma((3,)),
                dma((2, nz // 2, GRP)),
                dma((nz, GRP)),
                dma((nz, 2, GRP)),
                dma((GRP,)), dma((GRP,)),
                dma((QUAD,)), dma((QUAD,)),
                dma((3,)), dma((3,)),
            ],
            compiler_params=pltpu.CompilerParams(
                collective_id=0, has_side_effects=True, vmem_limit_bytes=40 * 2**20
            ),
            name="relay",
        )(
            x_in, stale_inputs, w_query, w_key, w_value, w_out, score_scale,
            assign.reshape(1, TILE),
        )

    return jax.shard_map(
        body,
        mesh=mesh,
        in_specs=(
            P("ctx", None),
            P("section", "ctx", None),
            P("section", None, None, None),
            P("section", None, None, None),
            P("section", None, None, None),
            P("section", None, None, None),
            P("section", None),
            P("ctx"),
        ),
        out_specs=P("section", "ctx", None),
        check_vma=False,
    )
```

```python
import functools
import math

import jax
import jax.numpy as jnp
from jax import lax
from jax.experimental import pallas as pl
from jax.experimental.pallas import tpu as pltpu
from jax.sharding import PartitionSpec as P

F32 = jnp.float32
BF16 = jnp.bfloat16
MESH = pl.DeviceIdType.MESH
EPS = 1e-6
HD = 128
TILE = 32
QUAD = 4
TOK = QUAD * TILE
GRP = 3
FEAT = QUAD * GRP * HD


def nn(a, b):
    return lax.dot_general(a, b, (((1,), (0,)), ((), ())), preferred_element_type=F32)


def nt(a, b):
    return lax.dot_general(a, b, (((1,), (1,)), ((), ())), preferred_element_type=F32)


def tn(a, b):
    return lax.dot_general(a, b, (((0,), (0,)), ((), ())), preferred_element_type=F32)


def arrived(ref, sem):
    pltpu.make_async_copy(ref, ref, sem).wait()


def kernel(
    sections, nz,
    x_ref, stale_ref, wq_ref, wk_ref, wv_ref, wo_ref, scale_ref, assign_ref,
    out_ref,
    stv, wts, normed, near, mask, xin, wk3, wT, wvoT, keys, vals, ht, ot, ob, sumsq, sumsq_out, mapped, raw,
    load_sem, xs_sem, xr_sem, ms_sem, mr_sem, qs_sem, qr_sem, ring_sem, sib_sem, near_sem,
    hs_sem, hr_sem, ss_sem, sr_sem, os_sem, or_sem,
):
    s = lax.axis_index("section")
    c = lax.axis_index("ctx")
    yh = c // (2 * nz)
    z = (c // 2) % nz
    core = c % 2
    half = nz // 2

    def at(section, y, zz, k):
        return (section, (y * nz + zz) * 2 + k)

    def peer(d):
        return (yh + d) % QUAD

    right = at(s, yh, (z + 1) % nz, core)
    left = at(s, yh, (z + nz - 1) % nz, core)
    sibling = at(s, yh, z, 1 - core)
    first = s == 0
    has_next = s < sections - 1
    mine = pl.ds(pl.multiple_of(yh * TILE, TILE), TILE)
    columns = pl.ds(pl.multiple_of(yh * (GRP * HD), GRP * HD), GRP * HD)

    def remote(src, dst, send, recv, device):
        return pltpu.make_async_remote_copy(
            src_ref=src, dst_ref=dst, send_sem=send, recv_sem=recv,
            device_id=device, device_id_type=MESH,
        )

    load_stale = pltpu.make_async_copy(stale_ref.at[0], stv, load_sem.at[0])
    load_stale.start()
    loads = []
    for i, w in enumerate((wk_ref, wq_ref, wv_ref, wo_ref)):
        loads.append(
            pltpu.make_async_copy(w.at[0, pl.ds(yh * GRP, GRP)], wts.at[i], load_sem.at[i + 1])
        )
        loads[-1].start()
    load_x = pltpu.make_async_copy(x_ref.at[:, columns], xin.at[mine, :], load_sem.at[5])

    @pl.when(first)
    def _():
        load_x.start()

    barrier = pltpu.get_barrier_semaphore()

    def greet(device):
        pl.semaphore_signal(barrier, inc=1, device_id=device, device_id_type=MESH)

    for d in range(1, QUAD):
        greet(at(s, peer(d), z, core))
    for device in (right, left, sibling):
        greet(device)

    @pl.when(has_next)
    def _():
        for d in range(QUAD):
            greet(at(s + 1, peer(d), z, core))

    @pl.when(s > 0)
    def _():
        for d in range(QUAD):
            greet(at(s - 1, peer(d), z, core))

    load_stale.wait()
    st = stv[...].astype(F32)
    n = (st * lax.rsqrt(jnp.mean(st * st, axis=-1, keepdims=True) + EPS)).astype(BF16)
    for h in range(QUAD * GRP):
        normed[h] = n[:, h * HD:(h + 1) * HD]
    near[0, 0, :, mine, :] = normed[pl.ds(yh * GRP, GRP)]

    row = assign_ref[...].astype(F32)
    row = jnp.concatenate([row] * QUAD, axis=1)
    lane = lax.broadcasted_iota(jnp.int32, (TILE, TOK), 1)
    sub = lax.broadcasted_iota(jnp.int32, (TILE, TOK), 0)
    rows = jnp.broadcast_to(row, (TILE, TOK))
    col = jnp.sum(jnp.where(lane == sub, rows, 0.0), axis=1, keepdims=True)
    fresh = jnp.where(col <= rows, 1.0, 0.0) * jnp.where(lane // TILE == yh, 1.0, 0.0)
    mask[mine, :] = fresh.astype(BF16)

    pl.semaphore_wait(
        barrier, 6 + QUAD * jnp.where(has_next, 1, 0) + QUAD * jnp.where(s > 0, 1, 0)
    )

    quad_sends, mask_sends, x_sends = [], [], []
    for d in range(1, QUAD):
        to = at(s, peer(d), z, core)
        quad_sends.append(remote(
            normed.at[pl.ds(peer(d) * GRP, GRP)], near.at[0, 0, :, mine, :],
            qs_sem.at[d - 1], qr_sem.at[d - 1], to,
        ))
        mask_sends.append(remote(
            mask.at[mine, :], mask.at[mine, :], ms_sem.at[d - 1], mr_sem.at[d - 1], to,
        ))
        x_sends.append(remote(
            x_ref.at[:, pl.ds(pl.multiple_of(peer(d) * (GRP * HD), GRP * HD), GRP * HD)],
            xin.at[mine, :], xs_sem.at[d - 1], xr_sem.at[d - 1], to,
        ))
    for copy in quad_sends:
        copy.start()

    @pl.when(first)
    def _():
        for copy in x_sends:
            copy.start()

    for copy in mask_sends:
        copy.start()

    for copy in loads:
        copy.wait()
    for h in range(GRP):
        wk = wts[0, h]
        wk3[h] = wk
        wvo = nn(wts[2, h], wts[3, h]).T.astype(BF16)
        wvoT[h] = wvo
        wT[h, 0:HD, :] = wts[1, h].astype(F32).T.astype(BF16)
        wT[h, HD:2 * HD, :] = wk.astype(F32).T.astype(BF16)
        wT[h, 2 * HD:, :] = wvo

    def to_right(t, h):
        return remote(
            near.at[(nz - t) % nz, 0, h], near.at[nz - t - 1, 0, h],
            ring_sem.at[0, t, h], near_sem.at[nz - t - 1, 0, h], right,
        )

    def to_left(t, h):
        return remote(
            near.at[t, 0, h], near.at[t + 1, 0, h],
            ring_sem.at[1, t, h], near_sem.at[t + 1, 0, h], left,
        )

    def to_sibling(r, h):
        return remote(
            near.at[r, 0, h], near.at[r, 1, h],
            sib_sem.at[r, h], near_sem.at[r, 1, h], sibling,
        )

    sends = []

    def start(copy):
        copy.start()
        sends.append(copy)

    def prepare(r, k):
        for h in range(GRP):
            block = near[r, k, h]
            raw = nn(block, wk3[h])
            scaled = raw * lax.rsqrt(jnp.mean(raw * raw, axis=-1, keepdims=True) + EPS)
            keys[h, r * TOK:(r + 1) * TOK, k * HD:(k + 1) * HD] = scaled.astype(BF16)
            vals[h, k * HD:(k + 1) * HD, r * TOK:(r + 1) * TOK] = nt(wvoT[h], block).astype(BF16)

    def sibling_slots(slots):
        for r in slots:
            for h in range(GRP):
                arrived(near.at[r, 1, h], near_sem.at[r, 1, h])
            prepare(r, 1)

    for d in range(1, QUAD):
        source = pl.ds(pl.multiple_of(((yh + QUAD - d) % QUAD) * TILE, TILE), TILE)
        arrived(near.at[0, 0, :, source, :], qr_sem.at[d - 1])
    for h in range(GRP):
        if half > 1 or h < 2:
            start(to_right(0, h))
        if half > 1 or h == 2:
            start(to_left(0, h))
        start(to_sibling(0, h))
    def sum_to(section, d):
        return remote(
            sumsq_out, sumsq.at[d], ss_sem.at[d], sr_sem.at[d], at(section, peer(d), z, core)
        )

    def squares(values):
        return jnp.sum((values * values).reshape(HD // 8, 8, TOK), axis=0)

    @pl.when(first)
    def _():
        load_x.wait()
        for d in range(1, QUAD):
            source = pl.ds(pl.multiple_of(((yh + QUAD - d) % QUAD) * TILE, TILE), TILE)
            arrived(xin.at[source, :], xr_sem.at[d - 1])
        part = jnp.zeros((8, TOK), F32)
        for h in range(GRP):
            turned = xin[:, h * HD:(h + 1) * HD].astype(F32).T
            ht[h] = turned.astype(BF16)
            part = part + squares(turned)
        sumsq_out[...] = part
        sumsq[0] = part
        own = [sum_to(s, d) for d in range(1, QUAD)]
        for copy in own:
            copy.start()
        for copy in own:
            copy.wait_send()

    prepare(0, 0)
    before = [0]
    for t in range(1, half + 1):
        back = nz - t
        for h in range(GRP):
            arrived(near.at[back, 0, h], near_sem.at[back, 0, h])
            if t < half - 1 or (t == half - 1 and h < 2):
                start(to_right(t, h))
            start(to_sibling(back, h))
            if back != t:
                arrived(near.at[t, 0, h], near_sem.at[t, 0, h])
                if t < half - 1 or (t == half - 1 and h == 2):
                    start(to_left(t, h))
                start(to_sibling(t, h))
        sibling_slots(before)
        before = [back] if back == t else [back, t]
        for r in before:
            prepare(r, 0)
    sibling_slots(before)

    for d in range(1, QUAD):
        source = pl.ds(pl.multiple_of(((yh + QUAD - d) % QUAD) * TILE, TILE), TILE)
        arrived(mask.at[source, :], mr_sem.at[d - 1])

    chosen = mask[...].astype(F32)
    keep = jnp.concatenate([1.0 - chosen, jnp.ones_like(chosen)], axis=1)
    zero = jnp.zeros((HD, TOK), BF16)
    for h in range(GRP):
        @pl.when(s > 0)
        def _():
            arrived(ht.at[h], hr_sem.at[h])

        both = nn(wT[h], ht[h])
        mapped[h] = both
        p = both[0:HD].astype(BF16)
        pair = jnp.concatenate(
            [jnp.concatenate([p, zero], axis=1), jnp.concatenate([zero, p], axis=1)], axis=0
        )
        raw[h] = nn(keys[h], pair)

    @pl.when(s > 0)
    def _():
        arrived(sumsq.at[0], sr_sem.at[0])

    for d in range(1, QUAD):
        arrived(sumsq.at[d], sr_sem.at[d])

    total = sumsq[0] + sumsq[1] + sumsq[2] + sumsq[3]
    mean_sq = jnp.sum(total, axis=0, keepdims=True) * (1.0 / FEAT) + EPS
    inv = lax.rsqrt(mean_sq)
    eps = EPS * mean_sq

    def hand_on(h):
        return remote(ot.at[h], ht.at[h], hs_sem.at[h], hr_sem.at[h], at(s + 1, yh, z, core))

    part = jnp.zeros((8, TOK), F32)
    for h in range(GRP):
        hidden = ht[h]
        pq, pk, pv = mapped[h, 0:HD], mapped[h, HD:2 * HD], mapped[h, 2 * HD:]
        scale = scale_ref[0, yh * GRP + h] * (math.log2(math.e) / math.sqrt(HD))
        aq = lax.rsqrt(jnp.sum(pq * pq, axis=0, keepdims=True) * (1.0 / HD) + eps) * scale
        bk = lax.rsqrt(jnp.sum(pk * pk, axis=0, keepdims=True) * (1.0 / HD) + eps)
        q = (pq * aq).astype(BF16)
        kf = (pk * bk).astype(BF16)
        vf = (pv * inv).astype(BF16)
        e = jnp.exp2(raw[h] * jnp.concatenate([aq, aq], axis=1))
        e = jnp.concatenate([e[0:TOK] * keep, e[TOK:]], axis=0)
        e_new = jnp.exp2(tn(kf, q)) * chosen
        den = jnp.sum(e.reshape(nz * TOK // 8, 8, 2 * TOK), axis=0)
        den = den[:, :TOK] + den[:, TOK:] + jnp.sum(e_new.reshape(TOK // 8, 8, TOK), axis=0)
        den = jnp.sum(den, axis=0, keepdims=True)
        both = nn(vals[h], e.astype(BF16))
        numer = both[0:HD, 0:TOK] + both[HD:, TOK:] + nn(vf, e_new.astype(BF16))
        result = (hidden.astype(F32) + numer * (1.0 / den)).astype(BF16)
        ot[h] = result

        @pl.when(has_next)
        def _():
            hand_on(h).start()

        part = part + squares(result.astype(F32))

    @pl.when(has_next)
    def _():
        sumsq_out[...] = part
        for d in (2, 1, 3, 0):
            sum_to(s + 1, d).start()

    for h in range(GRP):
        ob[:, h * HD:(h + 1) * HD] = ot[h].astype(F32).T.astype(BF16)
    own_out = pltpu.make_async_copy(ob.at[mine, :], out_ref.at[0, :, columns], load_sem.at[0])
    own_out.start()
    outs = []
    for d in range(1, QUAD):
        theirs = pl.ds(pl.multiple_of(peer(d) * TILE, TILE), TILE)
        outs.append(remote(
            ob.at[theirs, :], out_ref.at[0, :, columns],
            os_sem.at[d - 1], or_sem.at[d - 1], at(s, peer(d), z, core),
        ))
        outs[-1].start()

    for copy in sends + quad_sends + mask_sends:
        copy.wait_send()

    @pl.when(first)
    def _():
        for copy in x_sends:
            copy.wait_send()

    @pl.when(has_next)
    def _():
        for h in range(GRP):
            hand_on(h).wait_send()
        for d in range(QUAD):
            sum_to(s + 1, d).wait_send()

    own_out.wait()
    for d, copy in enumerate(outs, 1):
        copy.wait_send()
        theirs = pl.ds(
            pl.multiple_of(((yh + QUAD - d) % QUAD) * (GRP * HD), GRP * HD), GRP * HD
        )
        arrived(out_ref.at[0, :, theirs], or_sem.at[d - 1])


def solution(mesh):
    sections = mesh.shape["section"]
    nz = mesh.shape["ctx"] // (2 * QUAD)
    keys = nz * TOK

    def body(x_in, stale_inputs, w_query, w_key, w_value, w_out, score_scale, assign):
        anywhere = pl.BlockSpec(memory_space=pl.ANY)
        dma = pltpu.SemaphoreType.DMA
        return pl.pallas_call(
            functools.partial(kernel, sections, nz),
            out_shape=jax.ShapeDtypeStruct(stale_inputs.shape, BF16),
            in_specs=[anywhere] * 6 + [
                pl.BlockSpec(memory_space=pltpu.SMEM),
                pl.BlockSpec(memory_space=pltpu.VMEM),
            ],
            out_specs=anywhere,
            scratch_shapes=[
                pltpu.VMEM((TILE, FEAT), BF16),
                pltpu.VMEM((4, GRP, HD, HD), BF16),
                pltpu.VMEM((QUAD * GRP, TILE, HD), BF16),
                pltpu.VMEM((nz, 2, GRP, TOK, HD), BF16),
                pltpu.VMEM((TOK, TOK), BF16),
                pltpu.VMEM((TOK, GRP * HD), BF16),
                pltpu.VMEM((GRP, HD, HD), BF16),
                pltpu.VMEM((GRP, 3 * HD, HD), BF16),
                pltpu.VMEM((GRP, HD, HD), BF16),
                pltpu.VMEM((GRP, keys, 2 * HD), BF16),
                pltpu.VMEM((GRP, 2 * HD, keys), BF16),
                pltpu.VMEM((GRP, HD, TOK), BF16),
                pltpu.VMEM((GRP, HD, TOK), BF16),
                pltpu.VMEM((TOK, GRP * HD), BF16),
                pltpu.VMEM((QUAD, 8, TOK), F32),
                pltpu.VMEM((8, TOK), F32),
                pltpu.VMEM((GRP, 3 * HD, TOK), F32),
                pltpu.VMEM((GRP, keys, 2 * TOK), F32),
                dma((6,)),
                dma((3,)), dma((3,)),
                dma((3,)), dma((3,)),
                dma((3,)), dma((3,)),
                dma((2, nz // 2, GRP)),
                dma((nz, GRP)),
                dma((nz, 2, GRP)),
                dma((GRP,)), dma((GRP,)),
                dma((QUAD,)), dma((QUAD,)),
                dma((3,)), dma((3,)),
            ],
            compiler_params=pltpu.CompilerParams(
                collective_id=0, has_side_effects=True, vmem_limit_bytes=60 * 2**20
            ),
            name="relay",
        )(
            x_in, stale_inputs, w_query, w_key, w_value, w_out, score_scale,
            assign.reshape(1, TILE),
        )

    return jax.shard_map(
        body,
        mesh=mesh,
        in_specs=(
            P("ctx", None),
            P("section", "ctx", None),
            P("section", None, None, None),
            P("section", None, None, None),
            P("section", None, None, None),
            P("section", None, None, None),
            P("section", None),
            P("ctx"),
        ),
        out_specs=P("section", "ctx", None),
        check_vma=False,
    )
```

```python
import functools
import math

import jax
import jax.numpy as jnp
from jax import lax
from jax.experimental import pallas as pl
from jax.experimental.pallas import tpu as pltpu
from jax.sharding import PartitionSpec as P

F32 = jnp.float32
BF16 = jnp.bfloat16
MESH = pl.DeviceIdType.MESH
EPS = 1e-6
HD = 128
TILE = 32
QUAD = 4
TOK = QUAD * TILE
GRP = 3
FEAT = QUAD * GRP * HD


def nn(a, b):
    return lax.dot_general(a, b, (((1,), (0,)), ((), ())), preferred_element_type=F32)


def nt(a, b):
    return lax.dot_general(a, b, (((1,), (1,)), ((), ())), preferred_element_type=F32)


def tn(a, b):
    return lax.dot_general(a, b, (((0,), (0,)), ((), ())), preferred_element_type=F32)


def arrived(ref, sem):
    pltpu.make_async_copy(ref, ref, sem).wait()


def kernel(
    sections, nz,
    x_ref, stale_ref, wq_ref, wk_ref, wv_ref, wo_ref, scale_ref, assign_ref,
    out_ref,
    stv, wts, normed, near, mask, xin, wk3, wT, wvoT, keys, vals, ht, ot, ob, sumsq, sumsq_out, mapped, raw,
    load_sem, xs_sem, xr_sem, ms_sem, mr_sem, qs_sem, ring_sem, near_sem,
    hs_sem, hr_sem, ss_sem, sr_sem, os_sem, or_sem,
):
    s = lax.axis_index("section")
    c = lax.axis_index("ctx")
    yh = c // (2 * nz)
    z = (c // 2) % nz
    core = c % 2
    zh = z // 2
    m = (z % 2) * 2 + core

    def at(section, y, zz, k):
        return (section, (y * nz + zz) * 2 + k)

    def peer(d):
        return (m + d) % QUAD

    def mate(section, d):
        return at(section, yh, 2 * zh + peer(d) // 2, peer(d) % 2)

    def along(axis, step):
        if axis == 0:
            return at(s, (yh + QUAD + step) % QUAD, z, core)
        return at(s, yh, (z + nz + 2 * step) % nz, core)

    first = s == 0
    has_next = s < sections - 1
    mine = pl.ds(pl.multiple_of(m * TILE, TILE), TILE)
    columns = pl.ds(pl.multiple_of(m * (GRP * HD), GRP * HD), GRP * HD)

    def remote(src, dst, send, recv, device):
        return pltpu.make_async_remote_copy(
            src_ref=src, dst_ref=dst, send_sem=send, recv_sem=recv,
            device_id=device, device_id_type=MESH,
        )

    load_stale = pltpu.make_async_copy(stale_ref.at[0], stv, load_sem.at[0])
    load_stale.start()
    loads = []
    for i, w in enumerate((wk_ref, wq_ref, wv_ref, wo_ref)):
        loads.append(
            pltpu.make_async_copy(w.at[0, pl.ds(m * GRP, GRP)], wts.at[i], load_sem.at[i + 1])
        )
        loads[-1].start()
    load_x = pltpu.make_async_copy(x_ref.at[:, columns], xin.at[mine, :], load_sem.at[5])

    @pl.when(first)
    def _():
        load_x.start()

    barrier = pltpu.get_barrier_semaphore()

    def greet(device):
        pl.semaphore_signal(barrier, inc=1, device_id=device, device_id_type=MESH)

    for d in range(1, QUAD):
        greet(mate(s, d))
    for axis in range(2):
        greet(along(axis, 1))
        greet(along(axis, -1))

    @pl.when(has_next)
    def _():
        for d in range(QUAD):
            greet(mate(s + 1, d))

    @pl.when(s > 0)
    def _():
        for d in range(QUAD):
            greet(mate(s - 1, d))

    load_stale.wait()
    st = stv[...].astype(F32)
    n = (st * lax.rsqrt(jnp.mean(st * st, axis=-1, keepdims=True) + EPS)).astype(BF16)
    for h in range(QUAD * GRP):
        normed[h] = n[:, h * HD:(h + 1) * HD]
    near[0, 0, m] = normed[pl.ds(m * GRP, GRP)]

    row = assign_ref[...].astype(F32)
    row = jnp.concatenate([row] * QUAD, axis=1)
    lane = lax.broadcasted_iota(jnp.int32, (TILE, TOK), 1)
    sub = lax.broadcasted_iota(jnp.int32, (TILE, TOK), 0)
    rows = jnp.broadcast_to(row, (TILE, TOK))
    col = jnp.sum(jnp.where(lane == sub, rows, 0.0), axis=1, keepdims=True)
    fresh = jnp.where(col <= rows, 1.0, 0.0) * jnp.where(lane // TILE == m, 1.0, 0.0)
    mask[mine, :] = fresh.astype(BF16)

    pl.semaphore_wait(
        barrier, 7 + QUAD * jnp.where(has_next, 1, 0) + QUAD * jnp.where(s > 0, 1, 0)
    )

    quad_sends, mask_sends, x_sends = [], [], []
    for d in range(1, QUAD):
        to = mate(s, d)
        quad_sends.append(remote(
            normed.at[pl.ds(peer(d) * GRP, GRP)], near.at[0, 0, m],
            qs_sem.at[d - 1], near_sem.at[0, 0, m], to,
        ))
        mask_sends.append(remote(
            mask.at[mine, :], mask.at[mine, :], ms_sem.at[d - 1], mr_sem.at[d - 1], to,
        ))
        x_sends.append(remote(
            x_ref.at[:, pl.ds(pl.multiple_of(peer(d) * (GRP * HD), GRP * HD), GRP * HD)],
            xin.at[mine, :], xs_sem.at[d - 1], xr_sem.at[d - 1], to,
        ))
    for copy in quad_sends:
        copy.start()

    @pl.when(first)
    def _():
        for copy in x_sends:
            copy.start()

    for copy in mask_sends:
        copy.start()

    for copy in loads:
        copy.wait()
    for h in range(GRP):
        wk = wts[0, h]
        wk3[h] = wk
        wvo = nn(wts[2, h], wts[3, h]).T.astype(BF16)
        wvoT[h] = wvo
        wT[h, 0:HD, :] = wts[1, h].astype(F32).T.astype(BF16)
        wT[h, HD:2 * HD, :] = wk.astype(F32).T.astype(BF16)
        wT[h, 2 * HD:, :] = wvo

    sends = []

    def pass_on(ry, rz, j, axis, step):
        place = [ry, rz]
        place[axis] = (place[axis] - step) % QUAD
        copy = remote(
            near.at[ry, rz, j], near.at[place[0], place[1], j],
            ring_sem.at[len(sends)], near_sem.at[place[0], place[1], j], along(axis, step),
        )
        copy.start()
        sends.append(copy)

    def handle(far, near_by, j):
        one, two = (0, 1) if j < 2 else (1, 0)
        step = 1 - 2 * (j % 2)
        ry, rz = (far, near_by) if j < 2 else (near_by, far)
        if far or near_by:
            arrived(near.at[ry, rz, j], near_sem.at[ry, rz, j])
        if near_by == 0:
            if far == 0:
                pass_on(ry, rz, j, one, 1)
                pass_on(ry, rz, j, one, -1)
            elif (far + step) % QUAD == 0:
                pass_on(ry, rz, j, one, step)
            pass_on(ry, rz, j, two, 1)
            pass_on(ry, rz, j, two, -1)
        elif (near_by + step) % QUAD == 0:
            pass_on(ry, rz, j, two, step)

    def prepare(ry, rz):
        r, k = divmod(ry * QUAD + rz, 2)
        for h in range(GRP):
            block = near[ry, rz, :, h].reshape(TOK, HD)
            flat = nn(block, wk3[h])
            scaled = flat * lax.rsqrt(jnp.mean(flat * flat, axis=-1, keepdims=True) + EPS)
            keys[h, r * TOK:(r + 1) * TOK, k * HD:(k + 1) * HD] = scaled.astype(BF16)
            vals[h, k * HD:(k + 1) * HD, r * TOK:(r + 1) * TOK] = nt(wvoT[h], block).astype(BF16)

    for d in range(1, QUAD):
        source = (m + QUAD - d) % QUAD
        arrived(near.at[0, 0, source], near_sem.at[0, 0, source])
    for j in (0, 2, 1, 3):
        handle(0, 0, j)

    def sum_to(section, d):
        return remote(
            sumsq_out, sumsq.at[d], ss_sem.at[d], sr_sem.at[d], mate(section, d)
        )

    def squares(values):
        return jnp.sum((values * values).reshape(HD // 8, 8, TOK), axis=0)

    @pl.when(first)
    def _():
        load_x.wait()
        for d in range(1, QUAD):
            source = pl.ds(pl.multiple_of(((m + QUAD - d) % QUAD) * TILE, TILE), TILE)
            arrived(xin.at[source, :], xr_sem.at[d - 1])
        part = jnp.zeros((8, TOK), F32)
        for h in range(GRP):
            turned = xin[:, h * HD:(h + 1) * HD].astype(F32).T
            ht[h] = turned.astype(BF16)
            part = part + squares(turned)
        sumsq_out[...] = part
        sumsq[0] = part
        own = [sum_to(s, d) for d in range(1, QUAD)]
        for copy in own:
            copy.start()
        for copy in own:
            copy.wait_send()

    prepare(0, 0)
    rounds = (
        ((1, 0), (3, 0), (0, 1), (0, 3)),
        ((2, 0), (1, 1), (1, 3), (3, 1), (3, 3), (0, 2)),
        ((2, 1), (2, 3), (1, 2), (3, 2)),
        ((2, 2),),
    )
    come = {}
    for steps in rounds:
        for far, near_by in steps:
            for j in (0, 2, 1, 3):
                handle(far, near_by, j)
                place = (far, near_by) if j < 2 else (near_by, far)
                come[place] = come.get(place, 0) + 1
        for place in [p for p in come if come[p] == QUAD]:
            prepare(*place)
            del come[place]

    for d in range(1, QUAD):
        source = pl.ds(pl.multiple_of(((m + QUAD - d) % QUAD) * TILE, TILE), TILE)
        arrived(mask.at[source, :], mr_sem.at[d - 1])

    chosen = mask[...].astype(F32)
    keep = jnp.concatenate([1.0 - chosen, jnp.ones_like(chosen)], axis=1)
    zero = jnp.zeros((HD, TOK), BF16)
    def score(h):
        @pl.when(s > 0)
        def _():
            arrived(ht.at[h], hr_sem.at[h])

        both = nn(wT[h], ht[h])
        mapped[h] = both
        p = both[0:HD].astype(BF16)
        pair = jnp.concatenate(
            [jnp.concatenate([p, zero], axis=1), jnp.concatenate([zero, p], axis=1)], axis=0
        )
        raw[h] = nn(keys[h], pair)

    for h in range(GRP - 1):
        score(h)

    @pl.when(s > 0)
    def _():
        arrived(sumsq.at[0], sr_sem.at[0])

    for d in range(1, QUAD):
        arrived(sumsq.at[d], sr_sem.at[d])

    total = sumsq[0] + sumsq[1] + sumsq[2] + sumsq[3]
    mean_sq = jnp.sum(total, axis=0, keepdims=True) * (1.0 / FEAT) + EPS
    inv = lax.rsqrt(mean_sq)
    eps = EPS * mean_sq

    def hand_on(h):
        return remote(ot.at[h], ht.at[h], hs_sem.at[h], hr_sem.at[h], mate(s + 1, 0))

    part = jnp.zeros((8, TOK), F32)
    for h in range(GRP):
        if h == GRP - 1:
            score(h)
        hidden = ht[h]
        pq, pk, pv = mapped[h, 0:HD], mapped[h, HD:2 * HD], mapped[h, 2 * HD:]
        scale = scale_ref[0, m * GRP + h] * (math.log2(math.e) / math.sqrt(HD))
        aq = lax.rsqrt(jnp.sum(pq * pq, axis=0, keepdims=True) * (1.0 / HD) + eps) * scale
        bk = lax.rsqrt(jnp.sum(pk * pk, axis=0, keepdims=True) * (1.0 / HD) + eps)
        q = (pq * aq).astype(BF16)
        kf = (pk * bk).astype(BF16)
        vf = (pv * inv).astype(BF16)
        e = jnp.exp2(raw[h] * jnp.concatenate([aq, aq], axis=1))
        e = jnp.concatenate([e[0:TOK] * keep, e[TOK:]], axis=0)
        e_new = jnp.exp2(tn(kf, q)) * chosen
        den = jnp.sum(e.reshape(nz * TOK // 8, 8, 2 * TOK), axis=0)
        den = den[:, :TOK] + den[:, TOK:] + jnp.sum(e_new.reshape(TOK // 8, 8, TOK), axis=0)
        den = jnp.sum(den, axis=0, keepdims=True)
        both = nn(vals[h], e.astype(BF16))
        numer = both[0:HD, 0:TOK] + both[HD:, TOK:] + nn(vf, e_new.astype(BF16))
        result = (hidden.astype(F32) + numer * (1.0 / den)).astype(BF16)
        ot[h] = result

        @pl.when(has_next)
        def _():
            hand_on(h).start()

        part = part + squares(result.astype(F32))

    @pl.when(has_next)
    def _():
        sumsq_out[...] = part
        for d in (2, 1, 3, 0):
            sum_to(s + 1, d).start()

    for h in range(GRP):
        ob[:, h * HD:(h + 1) * HD] = ot[h].astype(F32).T.astype(BF16)
    own_out = pltpu.make_async_copy(ob.at[mine, :], out_ref.at[0, :, columns], load_sem.at[0])
    own_out.start()
    outs = []
    for d in range(1, QUAD):
        theirs = pl.ds(pl.multiple_of(peer(d) * TILE, TILE), TILE)
        outs.append(remote(
            ob.at[theirs, :], out_ref.at[0, :, columns],
            os_sem.at[d - 1], or_sem.at[d - 1], mate(s, d),
        ))
        outs[-1].start()

    for copy in sends + quad_sends + mask_sends:
        copy.wait_send()

    @pl.when(first)
    def _():
        for copy in x_sends:
            copy.wait_send()

    @pl.when(has_next)
    def _():
        for h in range(GRP):
            hand_on(h).wait_send()
        for d in range(QUAD):
            sum_to(s + 1, d).wait_send()

    own_out.wait()
    for d, copy in enumerate(outs, 1):
        copy.wait_send()
        theirs = pl.ds(
            pl.multiple_of(((m + QUAD - d) % QUAD) * (GRP * HD), GRP * HD), GRP * HD
        )
        arrived(out_ref.at[0, :, theirs], or_sem.at[d - 1])


def solution(mesh):
    sections = mesh.shape["section"]
    nz = mesh.shape["ctx"] // (2 * QUAD)
    keys = nz * TOK

    def body(x_in, stale_inputs, w_query, w_key, w_value, w_out, score_scale, assign):
        anywhere = pl.BlockSpec(memory_space=pl.ANY)
        dma = pltpu.SemaphoreType.DMA
        return pl.pallas_call(
            functools.partial(kernel, sections, nz),
            out_shape=jax.ShapeDtypeStruct(stale_inputs.shape, BF16),
            in_specs=[anywhere] * 6 + [
                pl.BlockSpec(memory_space=pltpu.SMEM),
                pl.BlockSpec(memory_space=pltpu.VMEM),
            ],
            out_specs=anywhere,
            scratch_shapes=[
                pltpu.VMEM((TILE, FEAT), BF16),
                pltpu.VMEM((4, GRP, HD, HD), BF16),
                pltpu.VMEM((QUAD * GRP, TILE, HD), BF16),
                pltpu.VMEM((QUAD, QUAD, QUAD, GRP, TILE, HD), BF16),
                pltpu.VMEM((TOK, TOK), BF16),
                pltpu.VMEM((TOK, GRP * HD), BF16),
                pltpu.VMEM((GRP, HD, HD), BF16),
                pltpu.VMEM((GRP, 3 * HD, HD), BF16),
                pltpu.VMEM((GRP, HD, HD), BF16),
                pltpu.VMEM((GRP, keys, 2 * HD), BF16),
                pltpu.VMEM((GRP, 2 * HD, keys), BF16),
                pltpu.VMEM((GRP, HD, TOK), BF16),
                pltpu.VMEM((GRP, HD, TOK), BF16),
                pltpu.VMEM((TOK, GRP * HD), BF16),
                pltpu.VMEM((QUAD, 8, TOK), F32),
                pltpu.VMEM((8, TOK), F32),
                pltpu.VMEM((GRP, 3 * HD, TOK), F32),
                pltpu.VMEM((GRP, keys, 2 * TOK), F32),
                dma((6,)),
                dma((3,)), dma((3,)),
                dma((3,)), dma((3,)),
                dma((3,)),
                dma((QUAD * 15,)),
                dma((QUAD, QUAD, QUAD)),
                dma((GRP,)), dma((GRP,)),
                dma((QUAD,)), dma((QUAD,)),
                dma((3,)), dma((3,)),
            ],
            compiler_params=pltpu.CompilerParams(
                collective_id=0, has_side_effects=True, vmem_limit_bytes=60 * 2**20
            ),
            name="relay",
        )(
            x_in, stale_inputs, w_query, w_key, w_value, w_out, score_scale,
            assign.reshape(1, TILE),
        )

    return jax.shard_map(
        body,
        mesh=mesh,
        in_specs=(
            P("ctx", None),
            P("section", "ctx", None),
            P("section", None, None, None),
            P("section", None, None, None),
            P("section", None, None, None),
            P("section", None, None, None),
            P("section", None),
            P("ctx"),
        ),
        out_specs=P("section", "ctx", None),
        check_vma=False,
    )
```

```python
import functools
import math

import jax
import jax.numpy as jnp
from jax import lax
from jax.experimental import pallas as pl
from jax.experimental.pallas import tpu as pltpu
from jax.sharding import PartitionSpec as P

F32 = jnp.float32
BF16 = jnp.bfloat16
MESH = pl.DeviceIdType.MESH
EPS = 1e-6
HD = 128
TILE = 32
QUAD = 4
TOK = QUAD * TILE
GRP = 3
FEAT = QUAD * GRP * HD


def nn(a, b):
    return lax.dot_general(a, b, (((1,), (0,)), ((), ())), preferred_element_type=F32)


def nt(a, b):
    return lax.dot_general(a, b, (((1,), (1,)), ((), ())), preferred_element_type=F32)


def tn(a, b):
    return lax.dot_general(a, b, (((0,), (0,)), ((), ())), preferred_element_type=F32)


def arrived(ref, sem):
    pltpu.make_async_copy(ref, ref, sem).wait()


def kernel(
    sections, nz,
    x_ref, stale_ref, wq_ref, wk_ref, wv_ref, wo_ref, scale_ref, assign_ref,
    out_ref,
    stv, wts, normed, near, mask, xin, wk3, wT, wvoT, keys, vals, ht, ot, ob, sumsq, sumsq_out, mapped, raw,
    tokens, queries, num_sum, den_sum,
    load_sem, xs_sem, xr_sem, ms_sem, mr_sem, qs_sem, ring_sem, near_sem,
    hs_sem, hr_sem, ss_sem, sr_sem, os_sem, or_sem, own_sem,
):
    s = lax.axis_index("section")
    c = lax.axis_index("ctx")
    yh = c // (2 * nz)
    z = (c // 2) % nz
    core = c % 2
    zh = z // 2
    m = (z % 2) * 2 + core

    def at(section, y, zz, k):
        return (section, (y * nz + zz) * 2 + k)

    def peer(d):
        return (m + d) % QUAD

    def mate(section, d):
        return at(section, yh, 2 * zh + peer(d) // 2, peer(d) % 2)

    late = s // (sections // 2)

    def along(axis, step, swap=late):
        on_y = swap if axis == 0 else 1 - swap
        return at(
            s, (yh + QUAD + step * on_y) % QUAD, (z + nz + 2 * step * (1 - on_y)) % nz, core
        )

    first = s == 0
    has_next = s < sections - 1
    mine = pl.ds(pl.multiple_of(m * TILE, TILE), TILE)
    columns = pl.ds(pl.multiple_of(m * (GRP * HD), GRP * HD), GRP * HD)

    def remote(src, dst, send, recv, device):
        return pltpu.make_async_remote_copy(
            src_ref=src, dst_ref=dst, send_sem=send, recv_sem=recv,
            device_id=device, device_id_type=MESH,
        )

    load_stale = pltpu.make_async_copy(stale_ref.at[0], stv, load_sem.at[0])
    load_stale.start()
    loads = []
    for i, w in enumerate((wk_ref, wq_ref, wv_ref, wo_ref)):
        loads.append(
            pltpu.make_async_copy(w.at[0, pl.ds(m * GRP, GRP)], wts.at[i], load_sem.at[i + 1])
        )
        loads[-1].start()
    load_x = pltpu.make_async_copy(x_ref.at[:, columns], xin.at[mine, :], load_sem.at[5])

    @pl.when(first)
    def _():
        load_x.start()

    barrier = pltpu.get_barrier_semaphore()

    def greet(device):
        pl.semaphore_signal(barrier, inc=1, device_id=device, device_id_type=MESH)

    for d in range(1, QUAD):
        greet(mate(s, d))
    for axis in range(2):
        greet(along(axis, 1))
        greet(along(axis, -1))

    @pl.when(has_next)
    def _():
        for d in range(QUAD):
            greet(mate(s + 1, d))

    @pl.when(s > 0)
    def _():
        for d in range(QUAD):
            greet(mate(s - 1, d))

    load_stale.wait()
    st = stv[...].astype(F32)
    n = (st * lax.rsqrt(jnp.mean(st * st, axis=-1, keepdims=True) + EPS)).astype(BF16)
    for h in range(QUAD * GRP):
        normed[h] = n[:, h * HD:(h + 1) * HD]
    near[0, 0, m] = normed[pl.ds(m * GRP, GRP)]

    row = assign_ref[...].astype(F32)
    row = jnp.concatenate([row] * QUAD, axis=1)
    lane = lax.broadcasted_iota(jnp.int32, (TILE, TOK), 1)
    sub = lax.broadcasted_iota(jnp.int32, (TILE, TOK), 0)
    rows = jnp.broadcast_to(row, (TILE, TOK))
    col = jnp.sum(jnp.where(lane == sub, rows, 0.0), axis=1, keepdims=True)
    fresh = jnp.where(col <= rows, 1.0, 0.0) * jnp.where(lane // TILE == m, 1.0, 0.0)
    mask[mine, :] = fresh.astype(BF16)

    pl.semaphore_wait(
        barrier, 7 + QUAD * jnp.where(has_next, 1, 0) + QUAD * jnp.where(s > 0, 1, 0)
    )

    quad_sends, mask_sends, x_sends = [], [], []
    for d in range(1, QUAD):
        to = mate(s, d)
        quad_sends.append(remote(
            normed.at[pl.ds(peer(d) * GRP, GRP)], near.at[0, 0, m],
            qs_sem.at[d - 1], near_sem.at[0, 0, m], to,
        ))
        mask_sends.append(remote(
            mask.at[mine, :], mask.at[mine, :], ms_sem.at[d - 1], mr_sem.at[d - 1], to,
        ))
        x_sends.append(remote(
            x_ref.at[:, pl.ds(pl.multiple_of(peer(d) * (GRP * HD), GRP * HD), GRP * HD)],
            xin.at[mine, :], xs_sem.at[d - 1], xr_sem.at[d - 1], to,
        ))
    for copy in quad_sends:
        copy.start()

    @pl.when(first)
    def _():
        for copy in x_sends:
            copy.start()

    for copy in mask_sends:
        copy.start()

    for copy in loads:
        copy.wait()
    for h in range(GRP):
        wk = wts[0, h]
        wk3[h] = wk
        wvo = nn(wts[2, h], wts[3, h]).T.astype(BF16)
        wvoT[h] = wvo
        wT[h, 0:HD, :] = wts[1, h].astype(F32).T.astype(BF16)
        wT[h, HD:2 * HD, :] = wk.astype(F32).T.astype(BF16)
        wT[h, 2 * HD:, :] = wvo

    sends = []

    def pass_on(far, near_by, j, axis, step):
        place = [far, near_by]
        place[axis] = (place[axis] - step) % QUAD
        copy = remote(
            near.at[far, near_by, j], near.at[place[0], place[1], j],
            ring_sem.at[len(sends)], near_sem.at[place[0], place[1], j],
            along(axis, step, (1 if j == 0 else late)),
        )
        copy.start()
        sends.append(copy)

    def handle(far, near_by, j):
        step = 1 - 2 * (j % 2)
        if far or near_by:
            arrived(near.at[far, near_by, j], near_sem.at[far, near_by, j])
        if near_by == 0:
            if far == 0:
                pass_on(far, near_by, j, 0, 1)
                pass_on(far, near_by, j, 0, -1)
            elif (far + step) % QUAD == 0:
                pass_on(far, near_by, j, 0, step)
            pass_on(far, near_by, j, 1, 1)
            pass_on(far, near_by, j, 1, -1)
        elif (near_by + step) % QUAD == 0:
            pass_on(far, near_by, j, 1, step)

    def prepare(ry, rz):
        r, k = divmod(ry * QUAD + rz, 2)
        for h in range(GRP):
            block = near[ry, rz, :, h].reshape(TOK, HD)
            flat = nn(block, wk3[h])
            scaled = flat * lax.rsqrt(jnp.mean(flat * flat, axis=-1, keepdims=True) + EPS)
            keys[h, r * TOK:(r + 1) * TOK, k * HD:(k + 1) * HD] = scaled.astype(BF16)
            vals[h, k * HD:(k + 1) * HD, r * TOK:(r + 1) * TOK] = nt(wvoT[h], block).astype(BF16)

        @pl.when(first)
        def _():
            for h in range(GRP):
                e = jnp.exp2(nn(keys[h, r * TOK:(r + 1) * TOK, k * HD:(k + 1) * HD], queries[h]))
                if ry == 0 and rz == 0:
                    e = e * (1.0 - mask[...].astype(F32))
                block_den = jnp.sum(e.reshape(TOK // 8, 8, TOK), axis=0)
                block_num = nn(
                    vals[h, k * HD:(k + 1) * HD, r * TOK:(r + 1) * TOK], e.astype(BF16)
                )
                if ry == 0 and rz == 0:
                    den_sum[h] = block_den
                    num_sum[h] = block_num
                else:
                    den_sum[h] = den_sum[h] + block_den
                    num_sum[h] = num_sum[h] + block_num

    for d in range(1, QUAD):
        source = (m + QUAD - d) % QUAD
        arrived(near.at[0, 0, source], near_sem.at[0, 0, source])
    for j in range(QUAD):
        handle(0, 0, j)

    def sum_to(section, d):
        return remote(
            sumsq_out, sumsq.at[d], ss_sem.at[d], sr_sem.at[d], mate(section, d)
        )

    def squares(values):
        return jnp.sum((values * values).reshape(HD // 8, 8, TOK), axis=0)

    @pl.when(first)
    def _():
        load_x.wait()
        for d in range(1, QUAD):
            source = pl.ds(pl.multiple_of(((m + QUAD - d) % QUAD) * TILE, TILE), TILE)
            arrived(xin.at[source, :], xr_sem.at[d - 1])
        part = jnp.zeros((8, TOK), F32)
        for h in range(GRP):
            turned = xin[:, h * HD:(h + 1) * HD].astype(F32).T
            ht[h] = turned.astype(BF16)
            part = part + squares(turned)
        sumsq_out[...] = part
        sumsq[0] = part
        for d in range(1, QUAD):
            sum_to(s, d).start()

    def set_scales():
        for d in range(1, QUAD):
            arrived(sumsq.at[d], sr_sem.at[d])
        total = sumsq[0] + sumsq[1] + sumsq[2] + sumsq[3]
        mean_sq = jnp.sum(total, axis=0, keepdims=True) * (1.0 / FEAT) + EPS
        tokens[0:1, :] = lax.rsqrt(mean_sq)
        tokens[1:2, :] = EPS * mean_sq

    def query_scale(h):
        pq = mapped[h, 0:HD]
        scale = scale_ref[0, m * GRP + h] * (math.log2(math.e) / math.sqrt(HD))
        eps = tokens[1:2, :]
        return lax.rsqrt(jnp.sum(pq * pq, axis=0, keepdims=True) * (1.0 / HD) + eps) * scale

    rounds = (
        ((1, 0), (3, 0), (0, 1), (0, 3)),
        ((2, 0), (1, 1), (1, 3), (3, 1), (3, 3), (0, 2)),
        ((2, 1), (2, 3), (1, 2), (3, 2)),
        ((2, 2),),
    )
    for steps in rounds:
        for far, near_by in steps:
            for j in range(QUAD):
                handle(far, near_by, j)
        if steps is rounds[0]:
            for d in range(1, QUAD):
                source = (m + QUAD - d) % QUAD
                source = pl.ds(pl.multiple_of(source * TILE, TILE), TILE)
                arrived(mask.at[source, :], mr_sem.at[d - 1])

            @pl.when(first)
            def _():
                set_scales()
                for d in range(1, QUAD):
                    sum_to(s, d).wait_send()
                for h in range(GRP):
                    mapped[h] = nn(wT[h], ht[h])
                    queries[h] = (mapped[h, 0:HD] * query_scale(h)).astype(BF16)

            prepare(0, 0)
        for far, near_by in steps:
            prepare(far, near_by)

    chosen = mask[...].astype(F32)
    keep = jnp.concatenate([1.0 - chosen, jnp.ones_like(chosen)], axis=1)
    zero = jnp.zeros((HD, TOK), BF16)

    def hand_on(h):
        return remote(ot.at[h], ht.at[h], hs_sem.at[h], hr_sem.at[h], mate(s + 1, 0))

    def out_columns(group, h):
        return pl.ds(pl.multiple_of(group * (GRP * HD) + h * HD, HD), HD)

    def out_rows(d):
        return pl.ds(pl.multiple_of(peer(d) * TILE, TILE), TILE)

    def own_out(h):
        return pltpu.make_async_copy(
            ob.at[h, mine, :], out_ref.at[0, :, out_columns(m, h)], own_sem.at[h]
        )

    def out_to(d, h):
        return remote(
            ob.at[h, out_rows(d), :], out_ref.at[0, :, out_columns(m, h)],
            os_sem.at[d - 1, h], or_sem.at[d - 1, h], mate(s, d),
        )

    def give_out(h):
        ob[h] = ot[h].astype(F32).T.astype(BF16)
        for d in (2, 1, 3):
            out_to(d, h).start()
        own_out(h).start()

    def score(h):
        arrived(ht.at[h], hr_sem.at[h])
        both = nn(wT[h], ht[h])
        mapped[h] = both
        p = both[0:HD].astype(BF16)
        pair = jnp.concatenate(
            [jnp.concatenate([p, zero], axis=1), jnp.concatenate([zero, p], axis=1)], axis=0
        )
        raw[h] = nn(keys[h], pair)

    def stale_part(h):
        aq = query_scale(h)
        e = jnp.exp2(raw[h] * jnp.concatenate([aq, aq], axis=1))
        e = jnp.concatenate([e[0:TOK] * keep, e[TOK:]], axis=0)
        den = jnp.sum(e.reshape(nz * TOK // 8, 8, 2 * TOK), axis=0)
        both = nn(vals[h], e.astype(BF16))
        return both[0:HD, 0:TOK] + both[HD:, TOK:], den[:, :TOK] + den[:, TOK:]

    def finish(h, numer, den):
        pq, pk, pv = mapped[h, 0:HD], mapped[h, HD:2 * HD], mapped[h, 2 * HD:]
        eps = tokens[1:2, :]
        bk = lax.rsqrt(jnp.sum(pk * pk, axis=0, keepdims=True) * (1.0 / HD) + eps)
        q = (pq * query_scale(h)).astype(BF16)
        kf = (pk * bk).astype(BF16)
        vf = (pv * tokens[0:1, :]).astype(BF16)
        e_new = jnp.exp2(tn(kf, q)) * chosen
        den = den + jnp.sum(e_new.reshape(TOK // 8, 8, TOK), axis=0)
        den = jnp.sum(den, axis=0, keepdims=True)
        numer = numer + nn(vf, e_new.astype(BF16))
        result = (ht[h].astype(F32) + numer * (1.0 / den)).astype(BF16)
        ot[h] = result
        part = squares(result.astype(F32))
        if h == 0:
            sumsq_out[...] = part
        else:
            sumsq_out[...] = sumsq_out[...] + part

        @pl.when(has_next)
        def _():
            hand_on(h).start()
            if h == GRP - 1:
                for d in (2, 1, 3, 0):
                    sum_to(s + 1, d).start()

    @pl.when(first)
    def _():
        for h in range(GRP):
            finish(h, num_sum[h], den_sum[h])

    @pl.when(s > 0)
    def _():
        for h in range(GRP - 1):
            score(h)
        arrived(sumsq.at[0], sr_sem.at[0])
        set_scales()
        for h in range(GRP):
            if h == GRP - 1:
                score(h)
            finish(h, *stale_part(h))

            @pl.when(jnp.logical_not(has_next))
            def _():
                give_out(h)

    @pl.when(has_next)
    def _():
        for h in range(GRP):
            give_out(h)

    for copy in sends + quad_sends + mask_sends:
        copy.wait_send()

    @pl.when(first)
    def _():
        for copy in x_sends:
            copy.wait_send()

    @pl.when(has_next)
    def _():
        for h in range(GRP):
            hand_on(h).wait_send()
        for d in range(QUAD):
            sum_to(s + 1, d).wait_send()

    for h in range(GRP):
        own_out(h).wait()
        for d in range(1, QUAD):
            out_to(d, h).wait_send()
            theirs = out_columns((m + QUAD - d) % QUAD, h)
            arrived(out_ref.at[0, :, theirs], or_sem.at[d - 1, h])


def solution(mesh):
    sections = mesh.shape["section"]
    nz = mesh.shape["ctx"] // (2 * QUAD)
    keys = nz * TOK

    def body(x_in, stale_inputs, w_query, w_key, w_value, w_out, score_scale, assign):
        anywhere = pl.BlockSpec(memory_space=pl.ANY)
        dma = pltpu.SemaphoreType.DMA
        return pl.pallas_call(
            functools.partial(kernel, sections, nz),
            out_shape=jax.ShapeDtypeStruct(stale_inputs.shape, BF16),
            in_specs=[anywhere] * 6 + [
                pl.BlockSpec(memory_space=pltpu.SMEM),
                pl.BlockSpec(memory_space=pltpu.VMEM),
            ],
            out_specs=anywhere,
            scratch_shapes=[
                pltpu.VMEM((TILE, FEAT), BF16),
                pltpu.VMEM((4, GRP, HD, HD), BF16),
                pltpu.VMEM((QUAD * GRP, TILE, HD), BF16),
                pltpu.VMEM((QUAD, QUAD, QUAD, GRP, TILE, HD), BF16),
                pltpu.VMEM((TOK, TOK), BF16),
                pltpu.VMEM((TOK, GRP * HD), BF16),
                pltpu.VMEM((GRP, HD, HD), BF16),
                pltpu.VMEM((GRP, 3 * HD, HD), BF16),
                pltpu.VMEM((GRP, HD, HD), BF16),
                pltpu.VMEM((GRP, keys, 2 * HD), BF16),
                pltpu.VMEM((GRP, 2 * HD, keys), BF16),
                pltpu.VMEM((GRP, HD, TOK), BF16),
                pltpu.VMEM((GRP, HD, TOK), BF16),
                pltpu.VMEM((GRP, TOK, HD), BF16),
                pltpu.VMEM((QUAD, 8, TOK), F32),
                pltpu.VMEM((8, TOK), F32),
                pltpu.VMEM((GRP, 3 * HD, TOK), F32),
                pltpu.VMEM((GRP, keys, 2 * TOK), F32),
                pltpu.VMEM((8, TOK), F32),
                pltpu.VMEM((GRP, HD, TOK), BF16),
                pltpu.VMEM((GRP, HD, TOK), F32),
                pltpu.VMEM((GRP, 8, TOK), F32),
                dma((6,)),
                dma((3,)), dma((3,)),
                dma((3,)), dma((3,)),
                dma((3,)),
                dma((QUAD * 15,)),
                dma((QUAD, QUAD, QUAD)),
                dma((GRP,)), dma((GRP,)),
                dma((QUAD,)), dma((QUAD,)),
                dma((3, GRP)), dma((3, GRP)), dma((GRP,)),
            ],
            compiler_params=pltpu.CompilerParams(
                collective_id=0, has_side_effects=True, vmem_limit_bytes=60 * 2**20
            ),
            name="relay",
        )(
            x_in, stale_inputs, w_query, w_key, w_value, w_out, score_scale,
            assign.reshape(1, TILE),
        )

    return jax.shard_map(
        body,
        mesh=mesh,
        in_specs=(
            P("ctx", None),
            P("section", "ctx", None),
            P("section", None, None, None),
            P("section", None, None, None),
            P("section", None, None, None),
            P("section", None, None, None),
            P("section", None),
            P("ctx"),
        ),
        out_specs=P("section", "ctx", None),
        check_vma=False,
    )
```

```python
import functools
import math

import jax
import jax.numpy as jnp
from jax import lax
from jax.experimental import pallas as pl
from jax.experimental.pallas import tpu as pltpu
from jax.sharding import PartitionSpec as P

F32 = jnp.float32
BF16 = jnp.bfloat16
MESH = pl.DeviceIdType.MESH
EPS = 1e-6
HD = 128
TILE = 32
QUAD = 4
TOK = QUAD * TILE
GRP = 3
FEAT = QUAD * GRP * HD


def nn(a, b):
    return lax.dot_general(a, b, (((1,), (0,)), ((), ())), preferred_element_type=F32)


def nt(a, b):
    return lax.dot_general(a, b, (((1,), (1,)), ((), ())), preferred_element_type=F32)


def tn(a, b):
    return lax.dot_general(a, b, (((0,), (0,)), ((), ())), preferred_element_type=F32)


def arrived(ref, sem):
    pltpu.make_async_copy(ref, ref, sem).wait()


def kernel(
    sections, nz,
    x_ref, stale_ref, wq_ref, wk_ref, wv_ref, wo_ref, scale_ref, assign_ref,
    out_ref,
    stv, wts, normed, near, mask, xin, wk3, wT, wvoT, keys, vals, ht, ot, ob, sumsq, sumsq_out, mapped, raw,
    tokens, queries, num_sum, den_sum,
    load_sem, xs_sem, xr_sem, ms_sem, mr_sem, qs_sem, ring_sem, near_sem,
    hs_sem, hr_sem, ss_sem, sr_sem, os_sem, or_sem, own_sem,
):
    s = lax.axis_index("section")
    c = lax.axis_index("ctx")
    yh = c // (2 * nz)
    z = (c // 2) % nz
    core = c % 2
    zh = z // 2
    m = (z % 2) * 2 + core

    def at(section, y, zz, k):
        return (section, (y * nz + zz) * 2 + k)

    def peer(d):
        return (m + d) % QUAD

    def mate(section, d):
        return at(section, yh, 2 * zh + peer(d) // 2, peer(d) % 2)

    late = s // (sections // 2)

    def along(axis, step, swap=late):
        on_y = swap if axis == 0 else 1 - swap
        return at(
            s, (yh + QUAD + step * on_y) % QUAD, (z + nz + 2 * step * (1 - on_y)) % nz, core
        )

    first = s == 0
    has_next = s < sections - 1
    mine = pl.ds(pl.multiple_of(m * TILE, TILE), TILE)
    columns = pl.ds(pl.multiple_of(m * (GRP * HD), GRP * HD), GRP * HD)

    def remote(src, dst, send, recv, device):
        return pltpu.make_async_remote_copy(
            src_ref=src, dst_ref=dst, send_sem=send, recv_sem=recv,
            device_id=device, device_id_type=MESH,
        )

    load_stale = pltpu.make_async_copy(stale_ref.at[0], stv, load_sem.at[0])
    load_stale.start()
    loads = []
    for i, w in enumerate((wk_ref, wq_ref, wv_ref, wo_ref)):
        loads.append(
            pltpu.make_async_copy(w.at[0, pl.ds(m * GRP, GRP)], wts.at[i], load_sem.at[i + 1])
        )
        loads[-1].start()
    load_x = pltpu.make_async_copy(x_ref.at[:, columns], xin.at[mine, :], load_sem.at[5])

    @pl.when(first)
    def _():
        load_x.start()

    barrier = pltpu.get_barrier_semaphore()

    def greet(device):
        pl.semaphore_signal(barrier, inc=1, device_id=device, device_id_type=MESH)

    for d in range(1, QUAD):
        greet(mate(s, d))
    for axis in range(2):
        greet(along(axis, 1))
        greet(along(axis, -1))

    @pl.when(has_next)
    def _():
        for d in range(QUAD):
            greet(mate(s + 1, d))

    @pl.when(s > 0)
    def _():
        for d in range(QUAD):
            greet(mate(s - 1, d))

    load_stale.wait()
    st = stv[...].astype(F32)
    n = (st * lax.rsqrt(jnp.mean(st * st, axis=-1, keepdims=True) + EPS)).astype(BF16)
    for h in range(QUAD * GRP):
        normed[h] = n[:, h * HD:(h + 1) * HD]
    near[0, 0, m] = normed[pl.ds(m * GRP, GRP)]

    row = assign_ref[...].astype(F32)
    row = jnp.concatenate([row] * QUAD, axis=1)
    lane = lax.broadcasted_iota(jnp.int32, (TILE, TOK), 1)
    sub = lax.broadcasted_iota(jnp.int32, (TILE, TOK), 0)
    rows = jnp.broadcast_to(row, (TILE, TOK))
    col = jnp.sum(jnp.where(lane == sub, rows, 0.0), axis=1, keepdims=True)
    fresh = jnp.where(col <= rows, 1.0, 0.0) * jnp.where(lane // TILE == m, 1.0, 0.0)
    mask[mine, :] = fresh.astype(BF16)

    pl.semaphore_wait(
        barrier, 7 + QUAD * jnp.where(has_next, 1, 0) + QUAD * jnp.where(s > 0, 1, 0)
    )

    quad_sends, mask_sends, x_sends = [], [], []
    for d in range(1, QUAD):
        to = mate(s, d)
        quad_sends.append(remote(
            normed.at[pl.ds(peer(d) * GRP, GRP)], near.at[0, 0, m],
            qs_sem.at[d - 1], near_sem.at[0, 0, m], to,
        ))
        mask_sends.append(remote(
            mask.at[mine, :], mask.at[mine, :], ms_sem.at[d - 1], mr_sem.at[d - 1], to,
        ))
        x_sends.append(remote(
            x_ref.at[:, pl.ds(pl.multiple_of(peer(d) * (GRP * HD), GRP * HD), GRP * HD)],
            xin.at[mine, :], xs_sem.at[d - 1], xr_sem.at[d - 1], to,
        ))
    for copy in quad_sends:
        copy.start()

    @pl.when(first)
    def _():
        for copy in x_sends:
            copy.start()

    for copy in mask_sends:
        copy.start()

    for copy in loads:
        copy.wait()
    for h in range(GRP):
        wk = wts[0, h]
        wk3[h] = wk
        wvo = nn(wts[2, h], wts[3, h]).T.astype(BF16)
        wvoT[h] = wvo
        wT[h, 0:HD, :] = wts[1, h].astype(F32).T.astype(BF16)
        wT[h, HD:2 * HD, :] = wk.astype(F32).T.astype(BF16)
        wT[h, 2 * HD:, :] = wvo

    sends = []

    def pass_on(far, near_by, d, axis, step):
        j = (m + QUAD - d) % QUAD
        place = [far, near_by]
        place[axis] = (place[axis] - step) % QUAD
        copy = remote(
            near.at[far, near_by, j], near.at[place[0], place[1], j],
            ring_sem.at[len(sends)], near_sem.at[place[0], place[1], j],
            along(axis, step, (1 if d == 0 else late)),
        )
        copy.start()
        sends.append(copy)

    def handle(far, near_by, d):
        j = (m + QUAD - d) % QUAD
        step = 1 - 2 * (d % 2)
        if far or near_by or d:
            arrived(near.at[far, near_by, j], near_sem.at[far, near_by, j])
        if near_by == 0:
            if far == 0:
                pass_on(far, near_by, d, 0, 1)
                pass_on(far, near_by, d, 0, -1)
            elif (far + step) % QUAD == 0:
                pass_on(far, near_by, d, 0, step)
            pass_on(far, near_by, d, 1, 1)
            pass_on(far, near_by, d, 1, -1)
        elif (near_by + step) % QUAD == 0:
            pass_on(far, near_by, d, 1, step)

    def prepare(ry, rz):
        r, k = divmod(ry * QUAD + rz, 2)
        for h in range(GRP):
            block = near[ry, rz, :, h].reshape(TOK, HD)
            flat = nn(block, wk3[h])
            scaled = flat * lax.rsqrt(jnp.mean(flat * flat, axis=-1, keepdims=True) + EPS)
            keys[h, r * TOK:(r + 1) * TOK, k * HD:(k + 1) * HD] = scaled.astype(BF16)
            vals[h, k * HD:(k + 1) * HD, r * TOK:(r + 1) * TOK] = nt(wvoT[h], block).astype(BF16)

        @pl.when(first)
        def _():
            for h in range(GRP):
                e = jnp.exp2(nn(keys[h, r * TOK:(r + 1) * TOK, k * HD:(k + 1) * HD], queries[h]))
                if ry == 0 and rz == 0:
                    e = e * (1.0 - mask[...].astype(F32))
                block_den = jnp.sum(e.reshape(TOK // 8, 8, TOK), axis=0)
                block_num = nn(
                    vals[h, k * HD:(k + 1) * HD, r * TOK:(r + 1) * TOK], e.astype(BF16)
                )
                if ry == 0 and rz == 0:
                    den_sum[h] = block_den
                    num_sum[h] = block_num
                else:
                    den_sum[h] = den_sum[h] + block_den
                    num_sum[h] = num_sum[h] + block_num

    for d in (0, 1, 3, 2):
        handle(0, 0, d)

    def sum_to(section, d):
        return remote(
            sumsq_out, sumsq.at[d], ss_sem.at[d], sr_sem.at[d], mate(section, d)
        )

    def squares(values):
        return jnp.sum(values * values, axis=0, keepdims=True)

    @pl.when(first)
    def _():
        load_x.wait()
        for d in range(1, QUAD):
            source = pl.ds(pl.multiple_of(((m + QUAD - d) % QUAD) * TILE, TILE), TILE)
            arrived(xin.at[source, :], xr_sem.at[d - 1])
        part = jnp.zeros((1, TOK), F32)
        for h in range(GRP):
            turned = xin[:, h * HD:(h + 1) * HD].astype(F32).T
            ht[h] = turned.astype(BF16)
            part = part + squares(turned)
        sumsq_out[...] = part
        sumsq[0] = part
        for d in range(1, QUAD):
            sum_to(s, d).start()

    def set_scales():
        for d in range(1, QUAD):
            arrived(sumsq.at[d], sr_sem.at[d])
        total = sumsq[0] + sumsq[1] + sumsq[2] + sumsq[3]
        mean_sq = total * (1.0 / FEAT) + EPS
        tokens[0:1, :] = lax.rsqrt(mean_sq)
        tokens[1:2, :] = EPS * mean_sq

    def query_scale(h):
        pq = mapped[h, 0:HD]
        scale = scale_ref[0, m * GRP + h] * (math.log2(math.e) / math.sqrt(HD))
        eps = tokens[1:2, :]
        return lax.rsqrt(jnp.sum(pq * pq, axis=0, keepdims=True) * (1.0 / HD) + eps) * scale

    rounds = (
        ((1, 0), (3, 0), (0, 1), (0, 3)),
        ((2, 0), (1, 1), (1, 3), (3, 1), (3, 3), (0, 2)),
        ((2, 1), (2, 3), (1, 2), (3, 2)),
        ((2, 2),),
    )
    for steps in rounds:
        for far, near_by in steps:
            for d in (0, 1, 3, 2):
                handle(far, near_by, d)
        if steps is rounds[0]:
            for d in range(1, QUAD):
                source = (m + QUAD - d) % QUAD
                source = pl.ds(pl.multiple_of(source * TILE, TILE), TILE)
                arrived(mask.at[source, :], mr_sem.at[d - 1])

            @pl.when(first)
            def _():
                set_scales()
                for d in range(1, QUAD):
                    sum_to(s, d).wait_send()
                for h in range(GRP):
                    mapped[h] = nn(wT[h], ht[h])
                    queries[h] = (mapped[h, 0:HD] * query_scale(h)).astype(BF16)

            prepare(0, 0)
        for far, near_by in steps:
            prepare(far, near_by)

    chosen = mask[...].astype(F32)
    keep = jnp.concatenate([1.0 - chosen, jnp.ones_like(chosen)], axis=1)
    zero = jnp.zeros((HD, TOK), BF16)

    def hand_on(h):
        return remote(ot.at[h], ht.at[h], hs_sem.at[h], hr_sem.at[h], mate(s + 1, 0))

    def out_columns(group, h):
        return pl.ds(pl.multiple_of(group * (GRP * HD) + h * HD, HD), HD)

    def out_rows(d):
        return pl.ds(pl.multiple_of(peer(d) * TILE, TILE), TILE)

    def own_out(h):
        return pltpu.make_async_copy(
            ob.at[h, mine, :], out_ref.at[0, :, out_columns(m, h)], own_sem.at[h]
        )

    def out_to(d, h):
        return remote(
            ob.at[h, out_rows(d), :], out_ref.at[0, :, out_columns(m, h)],
            os_sem.at[d - 1, h], or_sem.at[d - 1, h], mate(s, d),
        )

    def give_out(h):
        ob[h] = ot[h].astype(F32).T.astype(BF16)
        for d in (2, 1, 3):
            out_to(d, h).start()
        own_out(h).start()

    def score(h):
        arrived(ht.at[h], hr_sem.at[h])
        both = nn(wT[h], ht[h])
        mapped[h] = both
        p = both[0:HD].astype(BF16)
        pair = jnp.concatenate(
            [jnp.concatenate([p, zero], axis=1), jnp.concatenate([zero, p], axis=1)], axis=0
        )
        raw[h] = nn(keys[h], pair)

    def stale_part(h):
        aq = query_scale(h)
        e = jnp.exp2(raw[h] * jnp.concatenate([aq, aq], axis=1))
        e = jnp.concatenate([e[0:TOK] * keep, e[TOK:]], axis=0)
        den = jnp.sum(e.reshape(nz * TOK // 8, 8, 2 * TOK), axis=0)
        both = nn(vals[h], e.astype(BF16))
        return both[0:HD, 0:TOK] + both[HD:, TOK:], den[:, :TOK] + den[:, TOK:]

    def finish(h, numer, den):
        pq, pk, pv = mapped[h, 0:HD], mapped[h, HD:2 * HD], mapped[h, 2 * HD:]
        eps = tokens[1:2, :]
        bk = lax.rsqrt(jnp.sum(pk * pk, axis=0, keepdims=True) * (1.0 / HD) + eps)
        q = (pq * query_scale(h)).astype(BF16)
        kf = (pk * bk).astype(BF16)
        vf = (pv * tokens[0:1, :]).astype(BF16)
        e_new = jnp.exp2(tn(kf, q)) * chosen
        den = den + jnp.sum(e_new.reshape(TOK // 8, 8, TOK), axis=0)
        den = jnp.sum(den, axis=0, keepdims=True)
        numer = numer + nn(vf, e_new.astype(BF16))
        result = (ht[h].astype(F32) + numer * (1.0 / den)).astype(BF16)
        ot[h] = result
        part = squares(result.astype(F32))
        if h == 0:
            sumsq_out[...] = part
        else:
            sumsq_out[...] = sumsq_out[...] + part

        @pl.when(has_next)
        def _():
            if h == GRP - 1:
                for d in (2, 1, 3, 0):
                    sum_to(s + 1, d).start()
            hand_on(h).start()

    @pl.when(first)
    def _():
        for h in range(GRP):
            finish(h, num_sum[h], den_sum[h])

    @pl.when(s > 0)
    def _():
        for h in range(GRP - 1):
            score(h)
        arrived(sumsq.at[0], sr_sem.at[0])
        set_scales()
        for h in range(GRP):
            if h == GRP - 1:
                score(h)
            finish(h, *stale_part(h))

            @pl.when(jnp.logical_not(has_next))
            def _():
                give_out(h)

    @pl.when(has_next)
    def _():
        for h in range(GRP):
            give_out(h)

    for copy in sends + quad_sends + mask_sends:
        copy.wait_send()

    @pl.when(first)
    def _():
        for copy in x_sends:
            copy.wait_send()

    @pl.when(has_next)
    def _():
        for h in range(GRP):
            hand_on(h).wait_send()
        for d in range(QUAD):
            sum_to(s + 1, d).wait_send()

    for h in range(GRP):
        own_out(h).wait()
        for d in range(1, QUAD):
            out_to(d, h).wait_send()
            theirs = out_columns((m + QUAD - d) % QUAD, h)
            arrived(out_ref.at[0, :, theirs], or_sem.at[d - 1, h])


def solution(mesh):
    sections = mesh.shape["section"]
    nz = mesh.shape["ctx"] // (2 * QUAD)
    keys = nz * TOK

    def body(x_in, stale_inputs, w_query, w_key, w_value, w_out, score_scale, assign):
        anywhere = pl.BlockSpec(memory_space=pl.ANY)
        dma = pltpu.SemaphoreType.DMA
        return pl.pallas_call(
            functools.partial(kernel, sections, nz),
            out_shape=jax.ShapeDtypeStruct(stale_inputs.shape, BF16),
            in_specs=[anywhere] * 6 + [
                pl.BlockSpec(memory_space=pltpu.SMEM),
                pl.BlockSpec(memory_space=pltpu.VMEM),
            ],
            out_specs=anywhere,
            scratch_shapes=[
                pltpu.VMEM((TILE, FEAT), BF16),
                pltpu.VMEM((4, GRP, HD, HD), BF16),
                pltpu.VMEM((QUAD * GRP, TILE, HD), BF16),
                pltpu.VMEM((QUAD, QUAD, QUAD, GRP, TILE, HD), BF16),
                pltpu.VMEM((TOK, TOK), BF16),
                pltpu.VMEM((TOK, GRP * HD), BF16),
                pltpu.VMEM((GRP, HD, HD), BF16),
                pltpu.VMEM((GRP, 3 * HD, HD), BF16),
                pltpu.VMEM((GRP, HD, HD), BF16),
                pltpu.VMEM((GRP, keys, 2 * HD), BF16),
                pltpu.VMEM((GRP, 2 * HD, keys), BF16),
                pltpu.VMEM((GRP, HD, TOK), BF16),
                pltpu.VMEM((GRP, HD, TOK), BF16),
                pltpu.VMEM((GRP, TOK, HD), BF16),
                pltpu.VMEM((QUAD, 1, TOK), F32),
                pltpu.VMEM((1, TOK), F32),
                pltpu.VMEM((GRP, 3 * HD, TOK), F32),
                pltpu.VMEM((GRP, keys, 2 * TOK), F32),
                pltpu.VMEM((8, TOK), F32),
                pltpu.VMEM((GRP, HD, TOK), BF16),
                pltpu.VMEM((GRP, HD, TOK), F32),
                pltpu.VMEM((GRP, 8, TOK), F32),
                dma((6,)),
                dma((3,)), dma((3,)),
                dma((3,)), dma((3,)),
                dma((3,)),
                dma((QUAD * 15,)),
                dma((QUAD, QUAD, QUAD)),
                dma((GRP,)), dma((GRP,)),
                dma((QUAD,)), dma((QUAD,)),
                dma((3, GRP)), dma((3, GRP)), dma((GRP,)),
            ],
            compiler_params=pltpu.CompilerParams(
                collective_id=0, has_side_effects=True, vmem_limit_bytes=60 * 2**20
            ),
            name="relay",
        )(
            x_in, stale_inputs, w_query, w_key, w_value, w_out, score_scale,
            assign.reshape(1, TILE),
        )

    return jax.shard_map(
        body,
        mesh=mesh,
        in_specs=(
            P("ctx", None),
            P("section", "ctx", None),
            P("section", None, None, None),
            P("section", None, None, None),
            P("section", None, None, None),
            P("section", None, None, None),
            P("section", None),
            P("ctx"),
        ),
        out_specs=P("section", "ctx", None),
        check_vma=False,
    )
```

```python
import functools
import math

import jax
import jax.numpy as jnp
from jax import lax
from jax.experimental import pallas as pl
from jax.experimental.pallas import tpu as pltpu
from jax.sharding import PartitionSpec as P

F32 = jnp.float32
BF16 = jnp.bfloat16
MESH = pl.DeviceIdType.MESH
EPS = 1e-6
HD = 128
TILE = 32
QUAD = 4
TOK = QUAD * TILE
GRP = 3
FEAT = QUAD * GRP * HD


def nn(a, b):
    return lax.dot_general(a, b, (((1,), (0,)), ((), ())), preferred_element_type=F32)


def nt(a, b):
    return lax.dot_general(a, b, (((1,), (1,)), ((), ())), preferred_element_type=F32)


def tn(a, b):
    return lax.dot_general(a, b, (((0,), (0,)), ((), ())), preferred_element_type=F32)


def arrived(ref, sem):
    pltpu.make_async_copy(ref, ref, sem).wait()


def kernel(
    sections, nz,
    x_ref, stale_ref, wq_ref, wk_ref, wv_ref, wo_ref, scale_ref, assign_ref,
    out_ref,
    stv, wts, normed, near, mask, xin, wk3, wT, wvoT, keys, vals, ht, ot, ob, sumsq, sumsq_out, mapped, raw,
    tokens, queries, num_sum, den_sum,
    load_sem, xs_sem, xr_sem, ms_sem, mr_sem, qs_sem, ring_sem, near_sem,
    hs_sem, hr_sem, ss_sem, sr_sem, os_sem, or_sem, own_sem,
):
    s = lax.axis_index("section")
    c = lax.axis_index("ctx")
    yh = c // (2 * nz)
    z = (c // 2) % nz
    core = c % 2
    zh = z // 2
    m = (z % 2) * 2 + core

    def at(section, y, zz, k):
        return (section, (y * nz + zz) * 2 + k)

    def peer(d):
        return (m + d) % QUAD

    def mate(section, d):
        return at(section, yh, 2 * zh + peer(d) // 2, peer(d) % 2)

    late = s // (sections // 2)

    def along(axis, step, swap=late):
        on_y = swap if axis == 0 else 1 - swap
        return at(
            s, (yh + QUAD + step * on_y) % QUAD, (z + nz + 2 * step * (1 - on_y)) % nz, core
        )

    first = s == 0
    has_next = s < sections - 1
    mine = pl.ds(pl.multiple_of(m * TILE, TILE), TILE)
    columns = pl.ds(pl.multiple_of(m * (GRP * HD), GRP * HD), GRP * HD)

    def remote(src, dst, send, recv, device):
        return pltpu.make_async_remote_copy(
            src_ref=src, dst_ref=dst, send_sem=send, recv_sem=recv,
            device_id=device, device_id_type=MESH,
        )

    load_stale = pltpu.make_async_copy(stale_ref.at[0], stv, load_sem.at[0])
    load_stale.start()
    loads = []
    for i, w in enumerate((wk_ref, wq_ref, wv_ref, wo_ref)):
        loads.append(
            pltpu.make_async_copy(w.at[0, pl.ds(m * GRP, GRP)], wts.at[i], load_sem.at[i + 1])
        )
        loads[-1].start()
    load_x = pltpu.make_async_copy(x_ref.at[:, columns], xin.at[mine, :], load_sem.at[5])

    @pl.when(first)
    def _():
        load_x.start()

    barrier = pltpu.get_barrier_semaphore()

    def greet(device):
        pl.semaphore_signal(barrier, inc=1, device_id=device, device_id_type=MESH)

    for d in range(1, QUAD):
        greet(mate(s, d))
    for axis in range(2):
        greet(along(axis, 1))
        greet(along(axis, -1))

    @pl.when(has_next)
    def _():
        for d in range(QUAD):
            greet(mate(s + 1, d))

    @pl.when(s > 0)
    def _():
        for d in range(QUAD):
            greet(mate(s - 1, d))

    load_stale.wait()
    st = stv[...].astype(F32)
    n = (st * lax.rsqrt(jnp.mean(st * st, axis=-1, keepdims=True) + EPS)).astype(BF16)
    for h in range(QUAD * GRP):
        normed[h] = n[:, h * HD:(h + 1) * HD]
    near[0, 0, m] = normed[pl.ds(m * GRP, GRP)]

    row = assign_ref[...].astype(F32)
    row = jnp.concatenate([row] * QUAD, axis=1)
    lane = lax.broadcasted_iota(jnp.int32, (TILE, TOK), 1)
    sub = lax.broadcasted_iota(jnp.int32, (TILE, TOK), 0)
    rows = jnp.broadcast_to(row, (TILE, TOK))
    col = jnp.sum(jnp.where(lane == sub, rows, 0.0), axis=1, keepdims=True)
    fresh = jnp.where(col <= rows, 1.0, 0.0) * jnp.where(lane // TILE == m, 1.0, 0.0)
    mask[mine, :] = fresh.astype(BF16)

    pl.semaphore_wait(
        barrier, 7 + QUAD * jnp.where(has_next, 1, 0) + QUAD * jnp.where(s > 0, 1, 0)
    )

    quad_sends, mask_sends, x_sends = [], [], []
    for d in range(1, QUAD):
        to = mate(s, d)
        quad_sends.append(remote(
            normed.at[pl.ds(peer(d) * GRP, GRP)], near.at[0, 0, m],
            qs_sem.at[d - 1], near_sem.at[0, 0, m], to,
        ))
        mask_sends.append(remote(
            mask.at[mine, :], mask.at[mine, :], ms_sem.at[d - 1], mr_sem.at[d - 1], to,
        ))
        x_sends.append(remote(
            x_ref.at[:, pl.ds(pl.multiple_of(peer(d) * (GRP * HD), GRP * HD), GRP * HD)],
            xin.at[mine, :], xs_sem.at[d - 1], xr_sem.at[d - 1], to,
        ))
    for copy in quad_sends:
        copy.start()

    @pl.when(first)
    def _():
        for copy in x_sends:
            copy.start()

    for copy in mask_sends:
        copy.start()

    sends = []

    def pass_on(far, near_by, d, axis, step):
        j = (m + QUAD - d) % QUAD
        place = [far, near_by]
        place[axis] = (place[axis] - step) % QUAD
        copy = remote(
            near.at[far, near_by, j], near.at[place[0], place[1], j],
            ring_sem.at[len(sends)], near_sem.at[place[0], place[1], j],
            along(axis, step, (1 if d == 0 else late)),
        )
        copy.start()
        sends.append(copy)

    def handle(far, near_by, d):
        j = (m + QUAD - d) % QUAD
        step = 1 - 2 * (d % 2)
        if far or near_by or d:
            arrived(near.at[far, near_by, j], near_sem.at[far, near_by, j])
        if near_by == 0:
            if far == 0:
                pass_on(far, near_by, d, 0, 1)
                pass_on(far, near_by, d, 0, -1)
            elif (far + step) % QUAD == 0:
                pass_on(far, near_by, d, 0, step)
            pass_on(far, near_by, d, 1, 1)
            pass_on(far, near_by, d, 1, -1)
        elif (near_by + step) % QUAD == 0:
            pass_on(far, near_by, d, 1, step)

    def prepare(ry, rz):
        r, k = divmod(ry * QUAD + rz, 2)
        for h in range(GRP):
            block = near[ry, rz, :, h].reshape(TOK, HD)
            flat = nn(block, wk3[h])
            scaled = flat * lax.rsqrt(jnp.mean(flat * flat, axis=-1, keepdims=True) + EPS)
            keys[h, r * TOK:(r + 1) * TOK, k * HD:(k + 1) * HD] = scaled.astype(BF16)
            vals[h, k * HD:(k + 1) * HD, r * TOK:(r + 1) * TOK] = nt(wvoT[h], block).astype(BF16)

        @pl.when(first)
        def _():
            for h in range(GRP):
                e = jnp.exp2(nn(keys[h, r * TOK:(r + 1) * TOK, k * HD:(k + 1) * HD], queries[h]))
                if ry == 0 and rz == 0:
                    e = e * (1.0 - mask[...].astype(F32))
                block_den = jnp.sum(e.reshape(TOK // 8, 8, TOK), axis=0)
                block_num = nn(
                    vals[h, k * HD:(k + 1) * HD, r * TOK:(r + 1) * TOK], e.astype(BF16)
                )
                if ry == 0 and rz == 0:
                    den_sum[h] = block_den
                    num_sum[h] = block_num
                else:
                    den_sum[h] = den_sum[h] + block_den
                    num_sum[h] = num_sum[h] + block_num

    for d in (0, 1, 3, 2):
        handle(0, 0, d)

    for copy in loads:
        copy.wait()
    for h in range(GRP):
        wk = wts[0, h]
        wk3[h] = wk
        wvo = nn(wts[2, h], wts[3, h]).T.astype(BF16)
        wvoT[h] = wvo
        wT[h, 0:HD, :] = wts[1, h].astype(F32).T.astype(BF16)
        wT[h, HD:2 * HD, :] = wk.astype(F32).T.astype(BF16)
        wT[h, 2 * HD:, :] = wvo

    def sum_to(section, d):
        return remote(
            sumsq_out, sumsq.at[d], ss_sem.at[d], sr_sem.at[d], mate(section, d)
        )

    def squares(values):
        return jnp.sum(values * values, axis=0, keepdims=True)

    @pl.when(first)
    def _():
        load_x.wait()
        for d in range(1, QUAD):
            source = pl.ds(pl.multiple_of(((m + QUAD - d) % QUAD) * TILE, TILE), TILE)
            arrived(xin.at[source, :], xr_sem.at[d - 1])
        part = jnp.zeros((1, TOK), F32)
        for h in range(GRP):
            turned = xin[:, h * HD:(h + 1) * HD].astype(F32).T
            ht[h] = turned.astype(BF16)
            part = part + squares(turned)
        sumsq_out[...] = part
        sumsq[0] = part
        for d in range(1, QUAD):
            sum_to(s, d).start()

    def set_scales():
        for d in range(1, QUAD):
            arrived(sumsq.at[d], sr_sem.at[d])
        total = sumsq[0] + sumsq[1] + sumsq[2] + sumsq[3]
        mean_sq = total * (1.0 / FEAT) + EPS
        tokens[0:1, :] = lax.rsqrt(mean_sq)
        tokens[1:2, :] = EPS * mean_sq

    def query_scale(h):
        pq = mapped[h, 0:HD]
        scale = scale_ref[0, m * GRP + h] * (math.log2(math.e) / math.sqrt(HD))
        eps = tokens[1:2, :]
        return lax.rsqrt(jnp.sum(pq * pq, axis=0, keepdims=True) * (1.0 / HD) + eps) * scale

    rounds = (
        ((1, 0), (3, 0), (0, 1), (0, 3)),
        ((2, 0), (1, 1), (1, 3), (3, 1), (3, 3), (0, 2)),
        ((2, 1), (2, 3), (1, 2), (3, 2)),
        ((2, 2),),
    )
    for steps in rounds:
        for far, near_by in steps:
            for d in (0, 1, 3, 2):
                handle(far, near_by, d)
        if steps is rounds[0]:
            for d in range(1, QUAD):
                source = (m + QUAD - d) % QUAD
                source = pl.ds(pl.multiple_of(source * TILE, TILE), TILE)
                arrived(mask.at[source, :], mr_sem.at[d - 1])

            @pl.when(first)
            def _():
                set_scales()
                for d in range(1, QUAD):
                    sum_to(s, d).wait_send()
                for h in range(GRP):
                    mapped[h] = nn(wT[h], ht[h])
                    queries[h] = (mapped[h, 0:HD] * query_scale(h)).astype(BF16)

            prepare(0, 0)
        for far, near_by in steps:
            prepare(far, near_by)

    chosen = mask[...].astype(F32)
    keep = jnp.concatenate([1.0 - chosen, jnp.ones_like(chosen)], axis=1)
    zero = jnp.zeros((HD, TOK), BF16)

    def hand_on(h):
        return remote(ot.at[h], ht.at[h], hs_sem.at[h], hr_sem.at[h], mate(s + 1, 0))

    def out_columns(group, h):
        return pl.ds(pl.multiple_of(group * (GRP * HD) + h * HD, HD), HD)

    def out_rows(d):
        return pl.ds(pl.multiple_of(peer(d) * TILE, TILE), TILE)

    def own_out(h):
        return pltpu.make_async_copy(
            ob.at[h, mine, :], out_ref.at[0, :, out_columns(m, h)], own_sem.at[h]
        )

    def out_to(d, h):
        return remote(
            ob.at[h, out_rows(d), :], out_ref.at[0, :, out_columns(m, h)],
            os_sem.at[d - 1, h], or_sem.at[d - 1, h], mate(s, d),
        )

    def give_out(h):
        ob[h] = ot[h].astype(F32).T.astype(BF16)
        for d in (2, 1, 3):
            out_to(d, h).start()
        own_out(h).start()

    def score(h):
        arrived(ht.at[h], hr_sem.at[h])
        both = nn(wT[h], ht[h])
        mapped[h] = both
        p = both[0:HD].astype(BF16)
        pair = jnp.concatenate(
            [jnp.concatenate([p, zero], axis=1), jnp.concatenate([zero, p], axis=1)], axis=0
        )
        raw[h] = nn(keys[h], pair)

    def stale_part(h):
        aq = query_scale(h)
        e = jnp.exp2(raw[h] * jnp.concatenate([aq, aq], axis=1))
        e = jnp.concatenate([e[0:TOK] * keep, e[TOK:]], axis=0)
        den = jnp.sum(e.reshape(nz * TOK // 8, 8, 2 * TOK), axis=0)
        both = nn(vals[h], e.astype(BF16))
        return both[0:HD, 0:TOK] + both[HD:, TOK:], den[:, :TOK] + den[:, TOK:]

    def finish(h, numer, den):
        pq, pk, pv = mapped[h, 0:HD], mapped[h, HD:2 * HD], mapped[h, 2 * HD:]
        eps = tokens[1:2, :]
        bk = lax.rsqrt(jnp.sum(pk * pk, axis=0, keepdims=True) * (1.0 / HD) + eps)
        q = (pq * query_scale(h)).astype(BF16)
        kf = (pk * bk).astype(BF16)
        vf = (pv * tokens[0:1, :]).astype(BF16)
        e_new = jnp.exp2(tn(kf, q)) * chosen
        den = den + jnp.sum(e_new.reshape(TOK // 8, 8, TOK), axis=0)
        den = jnp.sum(den, axis=0, keepdims=True)
        numer = numer + nn(vf, e_new.astype(BF16))
        result = (ht[h].astype(F32) + numer * (1.0 / den)).astype(BF16)
        ot[h] = result
        part = squares(result.astype(F32))
        if h == 0:
            sumsq_out[...] = part
        else:
            sumsq_out[...] = sumsq_out[...] + part

        @pl.when(has_next)
        def _():
            if h == GRP - 1:
                for d in (2, 1, 3, 0):
                    sum_to(s + 1, d).start()
            hand_on(h).start()

    @pl.when(first)
    def _():
        for h in range(GRP):
            finish(h, num_sum[h], den_sum[h])

    @pl.when(s > 0)
    def _():
        for h in range(GRP - 1):
            score(h)
        arrived(sumsq.at[0], sr_sem.at[0])
        set_scales()
        for h in range(GRP):
            if h == GRP - 1:
                score(h)
            finish(h, *stale_part(h))

            @pl.when(jnp.logical_not(has_next))
            def _():
                give_out(h)

    @pl.when(has_next)
    def _():
        for h in range(GRP):
            give_out(h)

    for copy in sends + quad_sends + mask_sends:
        copy.wait_send()

    @pl.when(first)
    def _():
        for copy in x_sends:
            copy.wait_send()

    @pl.when(has_next)
    def _():
        for h in range(GRP):
            hand_on(h).wait_send()
        for d in range(QUAD):
            sum_to(s + 1, d).wait_send()

    for h in range(GRP):
        own_out(h).wait()
        for d in range(1, QUAD):
            out_to(d, h).wait_send()
            theirs = out_columns((m + QUAD - d) % QUAD, h)
            arrived(out_ref.at[0, :, theirs], or_sem.at[d - 1, h])


def solution(mesh):
    sections = mesh.shape["section"]
    nz = mesh.shape["ctx"] // (2 * QUAD)
    keys = nz * TOK

    def body(x_in, stale_inputs, w_query, w_key, w_value, w_out, score_scale, assign):
        anywhere = pl.BlockSpec(memory_space=pl.ANY)
        dma = pltpu.SemaphoreType.DMA
        return pl.pallas_call(
            functools.partial(kernel, sections, nz),
            out_shape=jax.ShapeDtypeStruct(stale_inputs.shape, BF16),
            in_specs=[anywhere] * 6 + [
                pl.BlockSpec(memory_space=pltpu.SMEM),
                pl.BlockSpec(memory_space=pltpu.VMEM),
            ],
            out_specs=anywhere,
            scratch_shapes=[
                pltpu.VMEM((TILE, FEAT), BF16),
                pltpu.VMEM((4, GRP, HD, HD), BF16),
                pltpu.VMEM((QUAD * GRP, TILE, HD), BF16),
                pltpu.VMEM((QUAD, QUAD, QUAD, GRP, TILE, HD), BF16),
                pltpu.VMEM((TOK, TOK), BF16),
                pltpu.VMEM((TOK, GRP * HD), BF16),
                pltpu.VMEM((GRP, HD, HD), BF16),
                pltpu.VMEM((GRP, 3 * HD, HD), BF16),
                pltpu.VMEM((GRP, HD, HD), BF16),
                pltpu.VMEM((GRP, keys, 2 * HD), BF16),
                pltpu.VMEM((GRP, 2 * HD, keys), BF16),
                pltpu.VMEM((GRP, HD, TOK), BF16),
                pltpu.VMEM((GRP, HD, TOK), BF16),
                pltpu.VMEM((GRP, TOK, HD), BF16),
                pltpu.VMEM((QUAD, 1, TOK), F32),
                pltpu.VMEM((1, TOK), F32),
                pltpu.VMEM((GRP, 3 * HD, TOK), F32),
                pltpu.VMEM((GRP, keys, 2 * TOK), F32),
                pltpu.VMEM((8, TOK), F32),
                pltpu.VMEM((GRP, HD, TOK), BF16),
                pltpu.VMEM((GRP, HD, TOK), F32),
                pltpu.VMEM((GRP, 8, TOK), F32),
                dma((6,)),
                dma((3,)), dma((3,)),
                dma((3,)), dma((3,)),
                dma((3,)),
                dma((QUAD * 15,)),
                dma((QUAD, QUAD, QUAD)),
                dma((GRP,)), dma((GRP,)),
                dma((QUAD,)), dma((QUAD,)),
                dma((3, GRP)), dma((3, GRP)), dma((GRP,)),
            ],
            compiler_params=pltpu.CompilerParams(
                collective_id=0, has_side_effects=True, vmem_limit_bytes=60 * 2**20
            ),
            name="relay",
        )(
            x_in, stale_inputs, w_query, w_key, w_value, w_out, score_scale,
            assign.reshape(1, TILE),
        )

    return jax.shard_map(
        body,
        mesh=mesh,
        in_specs=(
            P("ctx", None),
            P("section", "ctx", None),
            P("section", None, None, None),
            P("section", None, None, None),
            P("section", None, None, None),
            P("section", None, None, None),
            P("section", None),
            P("ctx"),
        ),
        out_specs=P("section", "ctx", None),
        check_vma=False,
    )
```

```python
import functools
import math

import jax
import jax.numpy as jnp
from jax import lax
from jax.experimental import pallas as pl
from jax.experimental.pallas import tpu as pltpu
from jax.sharding import PartitionSpec as P

F32 = jnp.float32
BF16 = jnp.bfloat16
MESH = pl.DeviceIdType.MESH
EPS = 1e-6
HD = 128
TILE = 32
QUAD = 4
TOK = QUAD * TILE
GRP = 3
FEAT = QUAD * GRP * HD


def nn(a, b):
    return lax.dot_general(a, b, (((1,), (0,)), ((), ())), preferred_element_type=F32)


def nt(a, b):
    return lax.dot_general(a, b, (((1,), (1,)), ((), ())), preferred_element_type=F32)


def tn(a, b):
    return lax.dot_general(a, b, (((0,), (0,)), ((), ())), preferred_element_type=F32)


def arrived(ref, sem):
    pltpu.make_async_copy(ref, ref, sem).wait()


def kernel(
    sections, nz,
    x_ref, stale_ref, wq_ref, wk_ref, wv_ref, wo_ref, scale_ref, assign_ref,
    out_ref,
    stv, wts, normed, near, mask, xin, wk3, wT, wvoT, keys, vals, ht, ot, ob, sumsq, sumsq_out, mapped, raw,
    tokens, queries, num_sum, den_sum,
    load_sem, xs_sem, xr_sem, ms_sem, mr_sem, qs_sem, ring_sem, near_sem,
    hs_sem, hr_sem, ss_sem, sr_sem, os_sem, or_sem, own_sem,
):
    s = lax.axis_index("section")
    c = lax.axis_index("ctx")
    yh = c // (2 * nz)
    z = (c // 2) % nz
    core = c % 2
    zh = z // 2
    m = (z % 2) * 2 + core

    def at(section, y, zz, k):
        return (section, (y * nz + zz) * 2 + k)

    def peer(d):
        return (m + d) % QUAD

    def mate(section, d):
        return at(section, yh, 2 * zh + peer(d) // 2, peer(d) % 2)

    late = s // (sections // 2)

    def along(axis, step, swap=late):
        on_y = swap if axis == 0 else 1 - swap
        return at(
            s, (yh + QUAD + step * on_y) % QUAD, (z + nz + 2 * step * (1 - on_y)) % nz, core
        )

    first = s == 0
    has_next = s < sections - 1
    mine = pl.ds(pl.multiple_of(m * TILE, TILE), TILE)
    columns = pl.ds(pl.multiple_of(m * (GRP * HD), GRP * HD), GRP * HD)

    def remote(src, dst, send, recv, device):
        return pltpu.make_async_remote_copy(
            src_ref=src, dst_ref=dst, send_sem=send, recv_sem=recv,
            device_id=device, device_id_type=MESH,
        )

    load_stale = pltpu.make_async_copy(stale_ref.at[0], stv, load_sem.at[0])
    load_stale.start()
    loads = []
    for i, w in enumerate((wk_ref, wq_ref, wv_ref, wo_ref)):
        loads.append(
            pltpu.make_async_copy(w.at[0, pl.ds(m * GRP, GRP)], wts.at[i], load_sem.at[i + 1])
        )
        loads[-1].start()
    load_x = pltpu.make_async_copy(x_ref.at[:, columns], xin.at[mine, :], load_sem.at[5])

    @pl.when(first)
    def _():
        load_x.start()

    barrier = pltpu.get_barrier_semaphore()

    def greet(device):
        pl.semaphore_signal(barrier, inc=1, device_id=device, device_id_type=MESH)

    for d in range(1, QUAD):
        greet(mate(s, d))
    for axis in range(2):
        greet(along(axis, 1))
        greet(along(axis, -1))

    @pl.when(has_next)
    def _():
        for d in range(QUAD):
            greet(mate(s + 1, d))

    @pl.when(s > 0)
    def _():
        for d in range(QUAD):
            greet(mate(s - 1, d))

    load_stale.wait()
    st = stv[...].astype(F32)
    n = (st * lax.rsqrt(jnp.mean(st * st, axis=-1, keepdims=True) + EPS)).astype(BF16)
    for h in range(QUAD * GRP):
        normed[h] = n[:, h * HD:(h + 1) * HD]
    near[0, 0, m] = normed[pl.ds(m * GRP, GRP)]

    row = assign_ref[...].astype(F32)
    row = jnp.concatenate([row] * QUAD, axis=1)
    lane = lax.broadcasted_iota(jnp.int32, (TILE, TOK), 1)
    sub = lax.broadcasted_iota(jnp.int32, (TILE, TOK), 0)
    rows = jnp.broadcast_to(row, (TILE, TOK))
    col = jnp.sum(jnp.where(lane == sub, rows, 0.0), axis=1, keepdims=True)
    fresh = jnp.where(col <= rows, 1.0, 0.0) * jnp.where(lane // TILE == m, 1.0, 0.0)
    mask[mine, :] = fresh.astype(BF16)

    pl.semaphore_wait(
        barrier, 7 + QUAD * jnp.where(has_next, 1, 0) + QUAD * jnp.where(s > 0, 1, 0)
    )

    quad_sends, mask_sends, x_sends = [], [], []
    for d in range(1, QUAD):
        to = mate(s, d)
        quad_sends.append(remote(
            normed.at[pl.ds(peer(d) * GRP, GRP)], near.at[0, 0, m],
            qs_sem.at[d - 1], near_sem.at[0, 0, m], to,
        ))
        mask_sends.append(remote(
            mask.at[mine, :], mask.at[mine, :], ms_sem.at[d - 1], mr_sem.at[d - 1], to,
        ))
        x_sends.append(remote(
            x_ref.at[:, pl.ds(pl.multiple_of(peer(d) * (GRP * HD), GRP * HD), GRP * HD)],
            xin.at[mine, :], xs_sem.at[d - 1], xr_sem.at[d - 1], to,
        ))
    for copy in quad_sends:
        copy.start()

    @pl.when(first)
    def _():
        for copy in x_sends:
            copy.start()

    for copy in mask_sends:
        copy.start()

    sends = []

    def pass_on(far, near_by, d, axis, step):
        j = (m + QUAD - d) % QUAD
        place = [far, near_by]
        place[axis] = (place[axis] - step) % QUAD
        copy = remote(
            near.at[far, near_by, j], near.at[place[0], place[1], j],
            ring_sem.at[len(sends)], near_sem.at[place[0], place[1], j],
            along(axis, step, (1 if d == 0 else late)),
        )
        copy.start()
        sends.append(copy)

    def handle(far, near_by, d):
        j = (m + QUAD - d) % QUAD
        step = 1 - 2 * (d % 2)
        if far or near_by or d:
            arrived(near.at[far, near_by, j], near_sem.at[far, near_by, j])
        if near_by == 0:
            pass_on(far, near_by, d, 1, 1)
            pass_on(far, near_by, d, 1, -1)
            if far == 0:
                pass_on(far, near_by, d, 0, 1)
                pass_on(far, near_by, d, 0, -1)
            elif (far + step) % QUAD == 0:
                pass_on(far, near_by, d, 0, step)
        elif (near_by + step) % QUAD == 0:
            pass_on(far, near_by, d, 1, step)

    def prepare(ry, rz):
        r, k = divmod(ry * QUAD + rz, 2)
        for h in range(GRP):
            block = near[ry, rz, :, h].reshape(TOK, HD)
            flat = nn(block, wk3[h])
            scaled = flat * lax.rsqrt(jnp.mean(flat * flat, axis=-1, keepdims=True) + EPS)
            keys[h, r * TOK:(r + 1) * TOK, k * HD:(k + 1) * HD] = scaled.astype(BF16)
            vals[h, k * HD:(k + 1) * HD, r * TOK:(r + 1) * TOK] = nt(wvoT[h], block).astype(BF16)

        @pl.when(first)
        def _():
            for h in range(GRP):
                e = jnp.exp2(nn(keys[h, r * TOK:(r + 1) * TOK, k * HD:(k + 1) * HD], queries[h]))
                if ry == 0 and rz == 0:
                    e = e * (1.0 - mask[...].astype(F32))
                block_den = jnp.sum(e.reshape(TOK // 8, 8, TOK), axis=0)
                block_num = nn(
                    vals[h, k * HD:(k + 1) * HD, r * TOK:(r + 1) * TOK], e.astype(BF16)
                )
                if ry == 0 and rz == 0:
                    den_sum[h] = block_den
                    num_sum[h] = block_num
                else:
                    den_sum[h] = den_sum[h] + block_den
                    num_sum[h] = num_sum[h] + block_num

    for d in (0, 1, 3, 2):
        handle(0, 0, d)

    for copy in loads:
        copy.wait()
    for h in range(GRP):
        wk = wts[0, h]
        wk3[h] = wk
        wvo = nn(wts[2, h], wts[3, h]).T.astype(BF16)
        wvoT[h] = wvo
        wT[h, 0:HD, :] = wts[1, h].astype(F32).T.astype(BF16)
        wT[h, HD:2 * HD, :] = wk.astype(F32).T.astype(BF16)
        wT[h, 2 * HD:, :] = wvo

    def sum_to(section, d):
        return remote(
            sumsq_out, sumsq.at[d], ss_sem.at[d], sr_sem.at[d], mate(section, d)
        )

    def squares(values):
        return jnp.sum(values * values, axis=0, keepdims=True)

    @pl.when(first)
    def _():
        load_x.wait()
        for d in range(1, QUAD):
            source = pl.ds(pl.multiple_of(((m + QUAD - d) % QUAD) * TILE, TILE), TILE)
            arrived(xin.at[source, :], xr_sem.at[d - 1])
        part = jnp.zeros((1, TOK), F32)
        for h in range(GRP):
            turned = xin[:, h * HD:(h + 1) * HD].astype(F32).T
            ht[h] = turned.astype(BF16)
            part = part + squares(turned)
        sumsq_out[...] = part
        sumsq[0] = part
        for d in range(1, QUAD):
            sum_to(s, d).start()

    def set_scales():
        for d in range(1, QUAD):
            arrived(sumsq.at[d], sr_sem.at[d])
        total = sumsq[0] + sumsq[1] + sumsq[2] + sumsq[3]
        mean_sq = total * (1.0 / FEAT) + EPS
        tokens[0:1, :] = lax.rsqrt(mean_sq)
        tokens[1:2, :] = EPS * mean_sq

    def query_scale(h):
        pq = mapped[h, 0:HD]
        scale = scale_ref[0, m * GRP + h] * (math.log2(math.e) / math.sqrt(HD))
        eps = tokens[1:2, :]
        return lax.rsqrt(jnp.sum(pq * pq, axis=0, keepdims=True) * (1.0 / HD) + eps) * scale

    rounds = (
        ((1, 0), (3, 0), (0, 1), (0, 3)),
        ((2, 0), (1, 1), (1, 3), (3, 1), (3, 3), (0, 2)),
        ((2, 1), (2, 3), (1, 2), (3, 2)),
        ((2, 2),),
    )
    for steps in rounds:
        for far, near_by in steps:
            for d in (0, 1, 3, 2):
                handle(far, near_by, d)
        if steps is rounds[0]:
            for d in range(1, QUAD):
                source = (m + QUAD - d) % QUAD
                source = pl.ds(pl.multiple_of(source * TILE, TILE), TILE)
                arrived(mask.at[source, :], mr_sem.at[d - 1])

            @pl.when(first)
            def _():
                set_scales()
                for d in range(1, QUAD):
                    sum_to(s, d).wait_send()
                for h in range(GRP):
                    mapped[h] = nn(wT[h], ht[h])
                    queries[h] = (mapped[h, 0:HD] * query_scale(h)).astype(BF16)

            prepare(0, 0)
        for far, near_by in steps:
            prepare(far, near_by)

    chosen = mask[...].astype(F32)
    keep = jnp.concatenate([1.0 - chosen, jnp.ones_like(chosen)], axis=1)
    zero = jnp.zeros((HD, TOK), BF16)

    def hand_on(h):
        return remote(ot.at[h], ht.at[h], hs_sem.at[h], hr_sem.at[h], mate(s + 1, 0))

    def out_columns(group, h):
        return pl.ds(pl.multiple_of(group * (GRP * HD) + h * HD, HD), HD)

    def out_rows(d):
        return pl.ds(pl.multiple_of(peer(d) * TILE, TILE), TILE)

    def own_out(h):
        return pltpu.make_async_copy(
            ob.at[h, mine, :], out_ref.at[0, :, out_columns(m, h)], own_sem.at[h]
        )

    def out_to(d, h):
        return remote(
            ob.at[h, out_rows(d), :], out_ref.at[0, :, out_columns(m, h)],
            os_sem.at[d - 1, h], or_sem.at[d - 1, h], mate(s, d),
        )

    def give_out(h):
        ob[h] = ot[h].astype(F32).T.astype(BF16)
        for d in (2, 1, 3):
            out_to(d, h).start()
        own_out(h).start()

    def score(h):
        arrived(ht.at[h], hr_sem.at[h])
        both = nn(wT[h], ht[h])
        mapped[h] = both
        p = both[0:HD].astype(BF16)
        pair = jnp.concatenate(
            [jnp.concatenate([p, zero], axis=1), jnp.concatenate([zero, p], axis=1)], axis=0
        )
        raw[h] = nn(keys[h], pair)

    def stale_part(h):
        aq = query_scale(h)
        e = jnp.exp2(raw[h] * jnp.concatenate([aq, aq], axis=1))
        e = jnp.concatenate([e[0:TOK] * keep, e[TOK:]], axis=0)
        den = jnp.sum(e.reshape(nz * TOK // 8, 8, 2 * TOK), axis=0)
        both = nn(vals[h], e.astype(BF16))
        return both[0:HD, 0:TOK] + both[HD:, TOK:], den[:, :TOK] + den[:, TOK:]

    def finish(h, numer, den):
        pq, pk, pv = mapped[h, 0:HD], mapped[h, HD:2 * HD], mapped[h, 2 * HD:]
        eps = tokens[1:2, :]
        bk = lax.rsqrt(jnp.sum(pk * pk, axis=0, keepdims=True) * (1.0 / HD) + eps)
        q = (pq * query_scale(h)).astype(BF16)
        kf = (pk * bk).astype(BF16)
        vf = (pv * tokens[0:1, :]).astype(BF16)
        e_new = jnp.exp2(tn(kf, q)) * chosen
        den = den + jnp.sum(e_new.reshape(TOK // 8, 8, TOK), axis=0)
        den = jnp.sum(den, axis=0, keepdims=True)
        numer = numer + nn(vf, e_new.astype(BF16))
        result = (ht[h].astype(F32) + numer * (1.0 / den)).astype(BF16)
        ot[h] = result
        part = squares(result.astype(F32))
        if h == 0:
            sumsq_out[...] = part
        else:
            sumsq_out[...] = sumsq_out[...] + part

        @pl.when(has_next)
        def _():
            if h == GRP - 1:
                for d in (2, 1, 3, 0):
                    sum_to(s + 1, d).start()
            hand_on(h).start()

    @pl.when(first)
    def _():
        for h in range(GRP):
            finish(h, num_sum[h], den_sum[h])

    @pl.when(s > 0)
    def _():
        for h in range(GRP - 1):
            score(h)
        arrived(sumsq.at[0], sr_sem.at[0])
        set_scales()
        for h in range(GRP):
            if h == GRP - 1:
                score(h)
            finish(h, *stale_part(h))

            @pl.when(jnp.logical_not(has_next))
            def _():
                give_out(h)

    @pl.when(has_next)
    def _():
        for h in range(GRP):
            give_out(h)

    for copy in sends + quad_sends + mask_sends:
        copy.wait_send()

    @pl.when(first)
    def _():
        for copy in x_sends:
            copy.wait_send()

    @pl.when(has_next)
    def _():
        for h in range(GRP):
            hand_on(h).wait_send()
        for d in range(QUAD):
            sum_to(s + 1, d).wait_send()

    for h in range(GRP):
        own_out(h).wait()
        for d in range(1, QUAD):
            out_to(d, h).wait_send()
            theirs = out_columns((m + QUAD - d) % QUAD, h)
            arrived(out_ref.at[0, :, theirs], or_sem.at[d - 1, h])


def solution(mesh):
    sections = mesh.shape["section"]
    nz = mesh.shape["ctx"] // (2 * QUAD)
    keys = nz * TOK

    def body(x_in, stale_inputs, w_query, w_key, w_value, w_out, score_scale, assign):
        anywhere = pl.BlockSpec(memory_space=pl.ANY)
        dma = pltpu.SemaphoreType.DMA
        return pl.pallas_call(
            functools.partial(kernel, sections, nz),
            out_shape=jax.ShapeDtypeStruct(stale_inputs.shape, BF16),
            in_specs=[anywhere] * 6 + [
                pl.BlockSpec(memory_space=pltpu.SMEM),
                pl.BlockSpec(memory_space=pltpu.VMEM),
            ],
            out_specs=anywhere,
            scratch_shapes=[
                pltpu.VMEM((TILE, FEAT), BF16),
                pltpu.VMEM((4, GRP, HD, HD), BF16),
                pltpu.VMEM((QUAD * GRP, TILE, HD), BF16),
                pltpu.VMEM((QUAD, QUAD, QUAD, GRP, TILE, HD), BF16),
                pltpu.VMEM((TOK, TOK), BF16),
                pltpu.VMEM((TOK, GRP * HD), BF16),
                pltpu.VMEM((GRP, HD, HD), BF16),
                pltpu.VMEM((GRP, 3 * HD, HD), BF16),
                pltpu.VMEM((GRP, HD, HD), BF16),
                pltpu.VMEM((GRP, keys, 2 * HD), BF16),
                pltpu.VMEM((GRP, 2 * HD, keys), BF16),
                pltpu.VMEM((GRP, HD, TOK), BF16),
                pltpu.VMEM((GRP, HD, TOK), BF16),
                pltpu.VMEM((GRP, TOK, HD), BF16),
                pltpu.VMEM((QUAD, 1, TOK), F32),
                pltpu.VMEM((1, TOK), F32),
                pltpu.VMEM((GRP, 3 * HD, TOK), F32),
                pltpu.VMEM((GRP, keys, 2 * TOK), F32),
                pltpu.VMEM((8, TOK), F32),
                pltpu.VMEM((GRP, HD, TOK), BF16),
                pltpu.VMEM((GRP, HD, TOK), F32),
                pltpu.VMEM((GRP, 8, TOK), F32),
                dma((6,)),
                dma((3,)), dma((3,)),
                dma((3,)), dma((3,)),
                dma((3,)),
                dma((QUAD * 15,)),
                dma((QUAD, QUAD, QUAD)),
                dma((GRP,)), dma((GRP,)),
                dma((QUAD,)), dma((QUAD,)),
                dma((3, GRP)), dma((3, GRP)), dma((GRP,)),
            ],
            compiler_params=pltpu.CompilerParams(
                collective_id=0, has_side_effects=True, vmem_limit_bytes=60 * 2**20
            ),
            name="relay",
        )(
            x_in, stale_inputs, w_query, w_key, w_value, w_out, score_scale,
            assign.reshape(1, TILE),
        )

    return jax.shard_map(
        body,
        mesh=mesh,
        in_specs=(
            P("ctx", None),
            P("section", "ctx", None),
            P("section", None, None, None),
            P("section", None, None, None),
            P("section", None, None, None),
            P("section", None, None, None),
            P("section", None),
            P("ctx"),
        ),
        out_specs=P("section", "ctx", None),
        check_vma=False,
    )
```
